32 devices in a mesh: bore: 8 (over y, x, core), freq: 4 (over z).
Axes of the slice: x: 2, y: 2, z: 4, core: 2. Of those that a mesh axis runs over, the one named last changes fastest.
Arguments:
- loads: bfloat16 [128, 64, 8192], P('bore', None, 'freq'), may hold values from -48 to 48
- pair_spectra: bfloat16 [8, 2, 4096, 4096], P('freq', None, 'bore'), may hold values from -0.09375 to 0.09375
- share: bfloat16 [128, 4096], P(None, 'bore'), may hold values from 0.5 to 2
- assignment: int32 [4096], replicated, may hold values from 0 to 63, as said below
- freq_index: int32 [8], replicated, may hold values from 1 to 4095
Outputs:
- wall_temps: bfloat16 [128, 64, 8192], P(('bore', 'freq'))
The draws below stay inside these ranges and needn't reach their ends.
Inputs may be any that keep to these rules, and one draw needn't show every extreme that they name: `assignment`: each of the 64 buildings is served by exactly 64 boreholes.
All inputs are finite; a program needn't handle non-finite values.
Results may differ from the reference program's by a relative error of at most 0.029.
Values may be sent and summed in bfloat16 or wider, within the bound.
A program may use at most 128 MiB of HBM per device.

```python
import math
import jax
import jax.numpy as jnp
from jax import lax

B = 4096
NBLD = 64
PER_BLD = 64
HOURS = 8192
F = 8
S = 128


def draw_assignment(key, part):
    order = jax.random.permutation(key, B)
    return (order % NBLD).astype(jnp.int32)


def set_ends(array, rng, smallest, largest):
    place = [jax.random.randint(jax.random.fold_in(rng, axis), (), 0, length) for axis, length in enumerate(array.shape)]
    widest = array.shape.index(max(array.shape))
    beside = place[:widest] + [(place[widest] + 1) % array.shape[widest]] + place[widest + 1:]
    return array.at[tuple(place)].set(smallest).at[tuple(beside)].set(largest)


def block_levels(own_key, dims, split, least, high):
    level = 1.0
    for dim, blocks in split:
        heights = jax.random.uniform(jax.random.fold_in(jax.random.fold_in(own_key, 6), dim), (blocks,), jnp.float32, least / len(split), high / len(split))
        level = level * jnp.repeat(jnp.exp(heights), dims[dim] // blocks).reshape((-1,) + (1,) * (len(dims) - 1 - dim))
    return level


def normal_values(rng, shape, scale, limit, cuts=(), held_as=jnp.bfloat16):
    entries = jax.random.normal(rng, shape, jnp.float32) * scale
    if len(cuts) > 0:
        entries = block_levels(rng, shape, cuts, -0.22, 0.18) * entries
    return jnp.clip(entries, min=-limit, max=limit).astype(held_as)


def setup_inputs(seed: int = 0) -> dict:
    key_of = jax.random.split(jax.random.key(seed), 6)
    return {
        "loads": normal_values(key_of[0], (S, NBLD, HOURS), 8.0, 48.0, ((0, 8), (2, 4))),
        "pair_spectra": normal_values(key_of[1], (F, 2, B, B), B ** -0.5, 0.09375, ((0, 4), (2, 8))),
        "share": jnp.clip(jnp.exp(math.log(2.0) - 1.3862944 * jax.random.uniform(key_of[2], (S, B), jnp.float32) ** block_levels(key_of[2], (S, B), ((1, 8),), -0.2, 0.2)), 0.5, 2.0).astype(jnp.bfloat16),
        "assignment": draw_assignment(jax.random.fold_in(key_of[5], 71), 0),
        "freq_index": set_ends(jax.random.randint(key_of[4], (F,), 1, HOURS // 2), jax.random.fold_in(key_of[4], 1), 1, (HOURS // 2) - 1).astype(jnp.int32),
    }


def tables(harmonics, hour_index):
    phase_idx = harmonics[:, None] * hour_index[None, :] % HOURS
    angles = phase_idx.astype(jnp.float32) * (2.0 * math.pi / HOURS)
    return (jnp.cos(angles), jnp.sin(angles))

def reference(loads, pair_spectra, share, assignment, freq_index):
    hour_index = jnp.arange(HOURS, dtype=jnp.int32)
    cos_table, sin_table = tables(freq_index, hour_index)

    def forward(scenario):
        series = scenario.astype(jnp.float32)
        real_part = jnp.dot(cos_table, series.T, precision=lax.Precision.HIGHEST)
        imag_part = -jnp.dot(sin_table, series.T, precision=lax.Precision.HIGHEST)
        return jnp.stack([real_part, imag_part], 0) / math.sqrt(HOURS)
    spectra = lax.map(forward, loads)
    building_spec = jnp.transpose(spectra, (2, 1, 0, 3)).astype(jnp.bfloat16)
    select = (assignment[None, :] == jnp.arange(NBLD, dtype=jnp.int32)[:, None]).astype(jnp.float32)
    share_wide = share.astype(jnp.float32)

    def superpose(operands):
        spec_freq, tiles = operands
        picked = jnp.einsum('csn,nj->csj', spec_freq.astype(jnp.float32), select, precision=lax.Precision.HIGHEST)
        source_spec = (picked * share_wide[None]).astype(jnp.bfloat16)
        crossed = jnp.einsum('csj,dij->cdsi', source_spec.astype(jnp.float32), tiles.astype(jnp.float32), precision=lax.Precision.HIGHEST)
        wall_spec = jnp.stack([crossed[0, 0] - crossed[1, 1], crossed[0, 1] + crossed[1, 0]], 0).astype(jnp.bfloat16)
        return jnp.einsum('csi,ni->csn', wall_spec.astype(jnp.float32), select, precision=lax.Precision.HIGHEST) / PER_BLD
    building_wall = lax.map(superpose, (building_spec, pair_spectra))
    per_scenario = jnp.transpose(building_wall, (2, 1, 0, 3))

    def inverse(spectra_block):
        summed = jnp.dot(cos_table.T, spectra_block[0], precision=lax.Precision.HIGHEST) - jnp.dot(sin_table.T, spectra_block[1], precision=lax.Precision.HIGHEST)
        return (summed.T / math.sqrt(F)).astype(jnp.bfloat16)
    return lax.map(inverse, per_scenario)
```

```python
import functools
import math

import jax
import jax.numpy as jnp
from jax import lax
from jax.experimental import pallas as pl
from jax.experimental.pallas import tpu as pltpu
from jax.sharding import PartitionSpec as P

NBLD = 64
FLOC = 2
MESH = pl.DeviceIdType.MESH
NT = (((1,), (1,)), ((), ()))
TN = (((0,), (0,)), ((), ()))


def harmonic_column(freq_ref, freqs):
    row = lax.broadcasted_iota(jnp.int32, (freqs, 1), 0)
    column = jnp.zeros((freqs, 1), jnp.int32)
    for k in range(freqs):
        column = jnp.where(row == k, freq_ref[k], column)
    return column


def cos_sin(harmonics, first_hour, count, hours, stride=1):
    freqs = harmonics.shape[0]
    t = lax.broadcasted_iota(jnp.int32, (freqs, count), 1) * stride + first_hour
    phase = (harmonics * t) & (hours - 1)
    quarter = hours // 4
    turn = (phase + quarter // 2) // quarter
    x = (phase - turn * quarter).astype(jnp.float32) * (2.0 * math.pi / hours)
    y = x * x
    c = 1.0 + y * (-0.5 + y * (1 / 24 + y * (-1 / 720 + y * (1 / 40320 - y * (1 / 3628800)))))
    s = x * (1.0 + y * (-1 / 6 + y * (1 / 120 + y * (-1 / 5040 + y * (1 / 362880)))))
    odd = (turn & 1) == 1
    cos = jnp.where(odd, s, c)
    sin = jnp.where(odd, c, s)
    cos = jnp.where((turn == 1) | (turn == 2), -cos, cos)
    sin = jnp.where((turn == 2) | (turn == 3), -sin, sin)
    return cos, sin


def halves(x):
    upper = x.astype(jnp.bfloat16)
    return upper, (x - upper.astype(jnp.float32)).astype(jnp.bfloat16)


def superpose_kernel(
    nb, nz, hours, freq_ref, owner_ref, loads_hbm, pair_hbm, share_hbm, out_ref,
    loads_v, pair_v, share_v, sel_v, grid_v, spec_v,
    rs_stage, rs_recv, bs_all, wall_stage, wall_recv, a_stage, a_recv,
    loads_sem, pair_sem, own_sem, sh_send, sh_recv, fw_send, fw_recv,
    rs_ssem, rs_rsem, bs_ssem, bs_rsem, wl_ssem, wl_rsem, a_ssem, a_rsem,
):
    b = lax.axis_index("bore")
    z = lax.axis_index("freq")
    sloc = loads_hbm.shape[0]
    tloc = loads_hbm.shape[2]
    freqs = freq_ref.shape[0]
    bores = owner_ref.shape[1]
    bloc = pair_hbm.shape[2]
    s4 = sloc // nz
    core = b % 2
    chip = b // 2
    chips = nb // 2
    sibling = b + 1 - 2 * core

    barrier = pltpu.get_barrier_semaphore()
    for r in range(1, nb):
        pl.semaphore_signal(barrier, inc=1, device_id=((b + r) % nb, z), device_id_type=MESH)
    for r in range(1, nz):
        pl.semaphore_signal(barrier, inc=1, device_id=(b, (z + r) % nz), device_id_type=MESH)

    parts = loads_sem.shape[0]
    sp = sloc // parts
    load_copies = [
        pltpu.make_async_copy(loads_hbm.at[pl.ds(i * sp, sp)], loads_v.at[pl.ds(i * sp, sp)], loads_sem.at[i])
        for i in range(parts)
    ]
    for copy in load_copies:
        copy.start()
    own_share = pltpu.make_async_copy(share_hbm, share_v.at[b], own_sem)
    own_share.start()
    pair_copies = [
        pltpu.make_async_copy(pair_hbm.at[f, d], pair_v.at[f, d], pair_sem.at[f, d])
        for f in range(FLOC)
        for d in range(2)
    ]

    cos, sin = cos_sin(harmonic_column(freq_ref, freqs), z * tloc, tloc, hours)
    table = jnp.concatenate([*halves(cos), *halves(sin)], 0)
    to = lax.broadcasted_iota(jnp.int32, (2 * freqs, 4 * freqs), 0)
    part = lax.broadcasted_iota(jnp.int32, (2 * freqs, 4 * freqs), 1)
    same = (to % freqs == part % freqs) & (to // freqs == part // (2 * freqs))
    join = jnp.where(same, jnp.where(to < freqs, 1.0, -1.0), 0.0).astype(jnp.bfloat16)

    pl.semaphore_wait(barrier, nb - 1 + nz - 1)

    share_copies = []
    for r in range(1, chips):
        share_copies.append(
            pltpu.make_async_remote_copy(
                src_ref=share_hbm, dst_ref=share_v.at[b], send_sem=sh_send.at[r], recv_sem=sh_recv.at[r],
                device_id=((chip + r) % chips * 2 + core, z), device_id_type=MESH,
            )
        )
    share_copies.append(
        pltpu.make_async_remote_copy(
            src_ref=share_hbm, dst_ref=share_v.at[b], send_sem=sh_send.at[0], recv_sem=sh_recv.at[0],
            device_id=(sibling, z), device_id_type=MESH,
        )
    )
    for copy in share_copies:
        copy.start()

    for i, copy in enumerate(load_copies):
        copy.wait()
        if i < len(pair_copies):
            pair_copies[i].start()
        chunk = loads_v[pl.ds(i * sp, sp)].reshape(sp * NBLD, tloc)
        x = lax.dot_general(chunk, table, NT, preferred_element_type=jnp.float32)
        upper, lower = halves(x)
        spec_v[:, pl.ds(i * sp * NBLD, sp * NBLD)] = (
            lax.dot_general(join, upper, NT, preferred_element_type=jnp.float32)
            + lax.dot_general(join, lower, NT, preferred_element_type=jnp.float32)
        ) * (1.0 / math.sqrt(hours))
    for copy in pair_copies[parts:]:
        copy.start()

    lanes = sloc * NBLD
    keep = lax.broadcasted_iota(jnp.int32, (sloc, lanes), 1) // NBLD == lax.broadcasted_iota(
        jnp.int32, (sloc, lanes), 0
    )
    fold_from = lax.broadcasted_iota(jnp.int32, (lanes, 128), 0) % NBLD
    fold_to = lax.broadcasted_iota(jnp.int32, (lanes, 128), 1)
    folded = jnp.zeros((nz * 2 * sloc, 128), jnp.float32)
    for f in range(FLOC):
        spread = jnp.concatenate(
            [
                jnp.where(keep, spec_v[pl.ds(c * freqs + k * FLOC + f, 1), :], 0.0).astype(jnp.bfloat16)
                for k in range(nz)
                for c in range(2)
            ],
            0,
        )
        fold = (fold_from + f * NBLD == fold_to).astype(jnp.float32).astype(jnp.bfloat16)
        folded = folded + jnp.dot(spread, fold, preferred_element_type=jnp.float32)
    rs_stage[...] = folded.astype(jnp.bfloat16).reshape(nz, 2 * sloc, 128)

    rs_copies = []
    for r in range(1, nz):
        to = (z + r) % nz
        rs_copies.append(
            pltpu.make_async_remote_copy(
                src_ref=rs_stage.at[to], dst_ref=rs_recv.at[z], send_sem=rs_ssem.at[r], recv_sem=rs_rsem.at[r],
                device_id=(b, to), device_id_type=MESH,
            )
        )
        rs_copies[-1].start()
    rs_recv[z] = rs_stage[z]

    for q in range(nb):
        piece = pl.ds(q * bloc, bloc)
        label = lax.broadcasted_iota(jnp.int32, (2 * NBLD, bloc), 0) % NBLD
        sel_v[:, piece] = (label == owner_ref[:, piece]).astype(jnp.float32).astype(jnp.bfloat16)

    here = sel_v[0:NBLD, pl.ds(pl.multiple_of(b * bloc, 128), bloc)]
    width = 1024

    def gather_rows(f):
        for d in range(2):
            pair_copies[2 * f + d].wait()

            def step(i, carry):
                piece = pl.ds(pl.multiple_of(i * width, width), width)
                total = jnp.dot(here, pair_v[f, d, :, piece], preferred_element_type=jnp.float32)
                grid_v[f, pl.ds(d * NBLD, NBLD), piece] = total.astype(jnp.bfloat16)
                return carry

            lax.fori_loop(0, bores // width, step, 0)

    gather_rows(0)

    for copy in rs_copies:
        copy.wait_recv()
    spec = rs_recv[0].astype(jnp.float32)
    for k in range(1, nz):
        spec = spec + rs_recv[k].astype(jnp.float32)
    bs_all[b] = spec.astype(jnp.bfloat16)
    bs_copies = []
    for r in range(1, nb):
        bs_copies.append(
            pltpu.make_async_remote_copy(
                src_ref=bs_all.at[b], dst_ref=bs_all.at[b], send_sem=bs_ssem.at[r], recv_sem=bs_rsem.at[r],
                device_id=((b + r) % nb, z), device_id_type=MESH,
            )
        )
        bs_copies[-1].start()

    fw_copies = []
    for r in range(1, chips):
        share_copies[r - 1].wait_recv()
        origin = (chip + chips - r) % chips * 2 + core
        fw_copies.append(
            pltpu.make_async_remote_copy(
                src_ref=share_v.at[origin], dst_ref=share_v.at[origin], send_sem=fw_send.at[r], recv_sem=fw_recv.at[r],
                device_id=(sibling, z), device_id_type=MESH,
            )
        )
        fw_copies[-1].start()

    gather_rows(1)

    own_share.wait()
    share_copies[-1].wait_recv()
    for copy in bs_copies:
        copy.wait_recv()
    for copy in fw_copies:
        copy.wait_recv()

    rows = nb * 2 * sloc
    spec_all = bs_all[...].reshape(rows, 128).astype(jnp.float32)
    half = lax.broadcasted_iota(jnp.int32, (rows, 128), 1) // NBLD
    spec_f = [jnp.where(half == f, spec_all, 0.0).astype(jnp.bfloat16) for f in range(FLOC)]

    def source_step(q, walls):
        piece = pl.ds(pl.multiple_of(q * bloc, 128), bloc)
        select = sel_v[:, piece]
        weight = share_v[q].astype(jnp.float32).reshape(nb, 1, sloc, bloc)
        new = []
        for f in range(FLOC):
            picked = jnp.dot(spec_f[f], select, preferred_element_type=jnp.float32)
            source = (picked.reshape(nb, 2, sloc, bloc) * weight).astype(jnp.bfloat16).reshape(rows, bloc)
            new.append(
                walls[f] + lax.dot_general(source, grid_v[f, :, piece], NT, preferred_element_type=jnp.float32)
            )
        return tuple(new)

    walls = lax.fori_loop(0, nb, source_step, tuple(jnp.zeros((rows, 128), jnp.float32) for _ in range(FLOC)), unroll=8)
    sign = jnp.where(lax.broadcasted_iota(jnp.int32, (nb * sloc, 128), 1) < NBLD, -1.0, 1.0)
    for f in range(FLOC):
        crossed = walls[f].reshape(nb, 2, sloc, 128)
        real = crossed[:, 0].reshape(nb * sloc, 128)
        imag = crossed[:, 1].reshape(nb * sloc, 128)
        joined = real + sign * pltpu.roll(imag, NBLD, 1)
        wall_stage[:, f] = joined.astype(jnp.bfloat16).reshape(nb, sloc, 128)

    wl_copies = []
    for r in range(1, nb):
        to = (b + r) % nb
        wl_copies.append(
            pltpu.make_async_remote_copy(
                src_ref=wall_stage.at[to], dst_ref=wall_recv.at[b], send_sem=wl_ssem.at[r], recv_sem=wl_rsem.at[r],
                device_id=(to, z), device_id_type=MESH,
            )
        )
        wl_copies[-1].start()
    wall_recv[b] = wall_stage[b]
    for copy in wl_copies:
        copy.wait_recv()
    wall = wall_recv[0].astype(jnp.float32)
    for q in range(1, nb):
        wall = wall + wall_recv[q].astype(jnp.float32)
    wall = wall * (NBLD / bores)
    for k in range(nz):
        for f in range(FLOC):
            a_stage[k, f * s4 : (f + 1) * s4, :] = wall[f, k * s4 : (k + 1) * s4, :]

    a_copies = []
    for r in range(1, nz):
        to = (z + r) % nz
        a_copies.append(
            pltpu.make_async_remote_copy(
                src_ref=a_stage.at[to], dst_ref=a_recv.at[z], send_sem=a_ssem.at[r], recv_sem=a_rsem.at[r],
                device_id=(b, to), device_id_type=MESH,
            )
        )
        a_copies[-1].start()
    a_recv[z] = a_stage[z]
    for copy in share_copies + rs_copies + bs_copies + fw_copies + wl_copies:
        copy.wait_send()
    for copy in a_copies:
        copy.wait()
    out_ref[...] = a_recv[...].reshape(nz * FLOC * s4, 128)


def superpose(loads, pair_spectra, share, owners, freq_index, nb, nz):
    sloc, _, tloc = loads.shape
    bloc, bores = pair_spectra.shape[2:]
    scenarios = share.shape[0]
    freqs = freq_index.shape[0]
    s4 = sloc // nz
    bf16, f32, dma = jnp.bfloat16, jnp.float32, pltpu.SemaphoreType.DMA
    anywhere = pl.BlockSpec(memory_space=pl.ANY)
    return pl.pallas_call(
        functools.partial(superpose_kernel, nb, nz, tloc * nz),
        out_shape=pltpu.VMEM((nz * FLOC * s4, 128), f32),
        in_specs=[
            pl.BlockSpec(memory_space=pltpu.SMEM),
            pl.BlockSpec(memory_space=pltpu.VMEM),
            anywhere,
            anywhere,
            anywhere,
        ],
        out_specs=pl.BlockSpec(memory_space=pltpu.VMEM),
        scratch_shapes=[
            pltpu.VMEM(loads.shape, bf16),
            pltpu.VMEM(pair_spectra.shape, bf16),
            pltpu.VMEM((nb, scenarios, bloc), bf16),
            pltpu.VMEM((2 * NBLD, bores), bf16),
            pltpu.VMEM((FLOC, 2 * NBLD, bores), bf16),
            pltpu.VMEM((2 * freqs, sloc * NBLD), f32),
            pltpu.VMEM((nz, 2 * sloc, 128), bf16),
            pltpu.VMEM((nz, 2 * sloc, 128), bf16),
            pltpu.VMEM((nb, 2 * sloc, 128), bf16),
            pltpu.VMEM((nb, FLOC, sloc, 128), bf16),
            pltpu.VMEM((nb, FLOC, sloc, 128), bf16),
            pltpu.VMEM((nz, FLOC * s4, 128), f32),
            pltpu.VMEM((nz, FLOC * s4, 128), f32),
            dma((4,)),
            dma((FLOC, 2)),
            dma,
            dma((nb // 2,)),
            dma((nb // 2,)),
            dma((nb // 2,)),
            dma((nb // 2,)),
            dma((nz,)),
            dma((nz,)),
            dma((nb,)),
            dma((nb,)),
            dma((nb,)),
            dma((nb,)),
            dma((nz,)),
            dma((nz,)),
        ],
        compiler_params=pltpu.CompilerParams(
            collective_id=0, has_side_effects=True, vmem_limit_bytes=56 * 2**20
        ),
        name="superpose",
    )(freq_index, owners, loads, pair_spectra, share)


def inverse_kernel(hours, freq_ref, wall_v, out_hbm, out_v, out_sem):
    freqs = freq_ref.shape[0]
    s4 = out_hbm.shape[0]
    parts = out_sem.shape[0]
    count = hours // parts
    harmonics = harmonic_column(freq_ref, freqs)
    base_cos, base_sin = cos_sin(harmonics, 0, count, hours)
    turn_cos, turn_sin = cos_sin(harmonics, 0, 128, hours, count)
    low = lax.broadcasted_iota(jnp.int32, (freqs, 128), 1) < NBLD
    real, imag = [], []
    for s in range(0, s4, 2):
        one = wall_v[pl.ds(s, freqs, stride=s4), :]
        two = wall_v[pl.ds(s + 1, freqs, stride=s4), :]
        real.append(jnp.where(low, one, pltpu.roll(two, NBLD, 1)))
        imag.append(jnp.where(low, pltpu.roll(one, NBLD, 1), two))
    left = jnp.concatenate([jnp.concatenate(real, 1), -jnp.concatenate(imag, 1)], 0)
    upper, lower = halves(left * (1.0 / math.sqrt(freqs)))
    upper, lower = upper.astype(jnp.float32), lower.astype(jnp.float32)
    left = jnp.concatenate([upper, upper, lower], 0).T.astype(jnp.bfloat16)
    width = min(512, count)
    copies = []
    for i in range(parts):
        c, s = turn_cos[:, i : i + 1], turn_sin[:, i : i + 1]
        for j in range(0, count, width):
            piece = slice(j, j + width)
            cos = base_cos[:, piece] * c - base_sin[:, piece] * s
            sin = base_sin[:, piece] * c + base_cos[:, piece] * s
            upper, lower = halves(jnp.concatenate([cos, sin], 0))
            right = jnp.concatenate([upper, lower, upper], 0)
            total = jnp.dot(left, right, preferred_element_type=jnp.float32)
            out_v[:, :, pl.ds(i * count + j, width)] = total.astype(jnp.bfloat16).reshape(s4, NBLD, width)
        piece = pl.ds(i * count, count)
        copies.append(pltpu.make_async_copy(out_v.at[:, :, piece], out_hbm.at[:, :, piece], out_sem.at[i]))
        copies[-1].start()
    for copy in copies:
        copy.wait()


def inverse(freq_index, wall, s4, hours):
    parts = 8
    return pl.pallas_call(
        functools.partial(inverse_kernel, hours),
        out_shape=jax.ShapeDtypeStruct((s4, NBLD, hours), jnp.bfloat16),
        in_specs=[pl.BlockSpec(memory_space=pltpu.SMEM), pl.BlockSpec(memory_space=pltpu.VMEM)],
        out_specs=pl.BlockSpec(memory_space=pl.ANY),
        scratch_shapes=[
            pltpu.VMEM((s4, NBLD, hours), jnp.bfloat16),
            pltpu.SemaphoreType.DMA((parts,)),
        ],
        compiler_params=pltpu.CompilerParams(vmem_limit_bytes=56 * 2**20),
        name="inverse",
    )(freq_index, pltpu.with_memory_space_constraint(wall, pltpu.VMEM))


def solution(mesh):
    nb, nz = mesh.shape["bore"], mesh.shape["freq"]

    def body(loads, pair_spectra, share, assignment, freq_index):
        owners = assignment.reshape(1, -1)
        wall = superpose(loads, pair_spectra, share, owners, freq_index, nb, nz)
        return inverse(freq_index, wall, loads.shape[0] // nz, loads.shape[2] * nz)

    return jax.shard_map(
        body,
        mesh=mesh,
        in_specs=(
            P("bore", None, "freq"),
            P("freq", None, "bore", None),
            P(None, "bore"),
            P(),
            P(),
        ),
        out_specs=P(("bore", "freq"), None, None),
        check_vma=False,
    )
```

```python
import functools
import math

import jax
import jax.numpy as jnp
from jax import lax
from jax.experimental import pallas as pl
from jax.experimental.pallas import tpu as pltpu
from jax.sharding import PartitionSpec as P

NBLD = 64
FLOC = 2
MESH = pl.DeviceIdType.MESH
NT = (((1,), (1,)), ((), ()))
TN = (((0,), (0,)), ((), ()))


def harmonic_column(freq_ref, freqs):
    row = lax.broadcasted_iota(jnp.int32, (freqs, 1), 0)
    column = jnp.zeros((freqs, 1), jnp.int32)
    for k in range(freqs):
        column = jnp.where(row == k, freq_ref[k], column)
    return column


def cos_sin(harmonics, first_hour, count, hours, stride=1):
    freqs = harmonics.shape[0]
    t = lax.broadcasted_iota(jnp.int32, (freqs, count), 1) * stride + first_hour
    phase = (harmonics * t) & (hours - 1)
    quarter = hours // 4
    turn = (phase + quarter // 2) // quarter
    x = (phase - turn * quarter).astype(jnp.float32) * (2.0 * math.pi / hours)
    y = x * x
    c = 1.0 + y * (-0.5 + y * (1 / 24 + y * (-1 / 720 + y * (1 / 40320 - y * (1 / 3628800)))))
    s = x * (1.0 + y * (-1 / 6 + y * (1 / 120 + y * (-1 / 5040 + y * (1 / 362880)))))
    odd = (turn & 1) == 1
    cos = jnp.where(odd, s, c)
    sin = jnp.where(odd, c, s)
    cos = jnp.where((turn == 1) | (turn == 2), -cos, cos)
    sin = jnp.where((turn == 2) | (turn == 3), -sin, sin)
    return cos, sin


def halves(x):
    upper = x.astype(jnp.bfloat16)
    return upper, (x - upper.astype(jnp.float32)).astype(jnp.bfloat16)


def superpose_kernel(
    nb, nz, hours, freq_ref, owner_ref, loads_hbm, pair_hbm, share_hbm, out_ref,
    loads_v, pair_v, share_v, sel_v, grid_v, cross_stage, cross_recv, spec_v,
    rs_stage, rs_recv, bs_stage, bs_all, wall_stage, wall_recv,
    loads_sem, pair_sem, own_sem, sh_send, sh_recv, fw_send, fw_recv,
    cr_ssem, cr_rsem, rs_ssem, rs_rsem, bs_ssem, bs_rsem, wl_ssem, wl_rsem,
):
    b = lax.axis_index("bore")
    z = lax.axis_index("freq")
    sloc = loads_hbm.shape[0]
    tloc = loads_hbm.shape[2]
    freqs = freq_ref.shape[0]
    bores = owner_ref.shape[1]
    bloc = pair_hbm.shape[2]
    scenarios = share_hbm.shape[0]
    s4 = sloc // nz
    core = b % 2
    chip = b // 2
    chips = nb // 2
    sibling = b + 1 - 2 * core
    near_first = sorted(
        ((r, k) for r in range(nb) for k in range(nz) if r or k), key=lambda rk: min(rk[1], nz - rk[1])
    )

    barrier = pltpu.get_barrier_semaphore()
    for r, k in near_first:
        pl.semaphore_signal(barrier, inc=1, device_id=((b + r) % nb, (z + k) % nz), device_id_type=MESH)

    parts = loads_sem.shape[0]
    sp = sloc // parts
    load_copies = [
        pltpu.make_async_copy(loads_hbm.at[pl.ds(i * sp, sp)], loads_v.at[pl.ds(i * sp, sp)], loads_sem.at[i])
        for i in range(parts)
    ]
    for copy in load_copies:
        copy.start()
    own_share = pltpu.make_async_copy(share_hbm, share_v.at[b], own_sem)
    own_share.start()
    turns = (1 - core, core)
    pair_copies = [
        pltpu.make_async_copy(pair_hbm.at[turns[i], d], pair_v.at[turns[i], d], pair_sem.at[i, d])
        for i in range(FLOC)
        for d in range(2)
    ]

    cos, sin = cos_sin(harmonic_column(freq_ref, freqs), z * tloc, tloc, hours)
    table = jnp.concatenate([*halves(cos), *halves(sin)], 0)
    to = lax.broadcasted_iota(jnp.int32, (2 * freqs, 4 * freqs), 0)
    part = lax.broadcasted_iota(jnp.int32, (2 * freqs, 4 * freqs), 1)
    same = (to % freqs == part % freqs) & (to // freqs == part // (2 * freqs))
    join = jnp.where(same, jnp.where(to < freqs, 1.0, -1.0), 0.0).astype(jnp.bfloat16)

    pl.semaphore_wait(barrier, nb * nz - 1)

    share_copies = []
    for r in range(1, chips):
        share_copies.append(
            pltpu.make_async_remote_copy(
                src_ref=share_hbm, dst_ref=share_v.at[b], send_sem=sh_send.at[r], recv_sem=sh_recv.at[r],
                device_id=((chip + r) % chips * 2 + core, z), device_id_type=MESH,
            )
        )
    share_copies.append(
        pltpu.make_async_remote_copy(
            src_ref=share_hbm, dst_ref=share_v.at[b], send_sem=sh_send.at[0], recv_sem=sh_recv.at[0],
            device_id=(sibling, z), device_id_type=MESH,
        )
    )
    for copy in share_copies:
        copy.start()

    for i, copy in enumerate(load_copies):
        copy.wait()
        if i < len(pair_copies):
            pair_copies[i].start()
        chunk = loads_v[pl.ds(i * sp, sp)].reshape(sp * NBLD, tloc)
        x = lax.dot_general(chunk, table, NT, preferred_element_type=jnp.float32)
        upper, lower = halves(x)
        spec_v[:, pl.ds(i * sp * NBLD, sp * NBLD)] = (
            lax.dot_general(join, upper, NT, preferred_element_type=jnp.float32)
            + lax.dot_general(join, lower, NT, preferred_element_type=jnp.float32)
        ) * (1.0 / math.sqrt(hours))
    for copy in pair_copies[parts:]:
        copy.start()

    lanes = sloc * NBLD
    keep = lax.broadcasted_iota(jnp.int32, (sloc, lanes), 1) // NBLD == lax.broadcasted_iota(
        jnp.int32, (sloc, lanes), 0
    )
    fold_from = lax.broadcasted_iota(jnp.int32, (lanes, 128), 0) % NBLD
    fold_to = lax.broadcasted_iota(jnp.int32, (lanes, 128), 1)
    folded = jnp.zeros((freqs * sloc, 128), jnp.float32)
    for c in range(2):
        spread = jnp.concatenate(
            [
                jnp.where(keep, spec_v[pl.ds(c * freqs + k, 1), :], 0.0).astype(jnp.bfloat16)
                for k in range(freqs)
            ],
            0,
        )
        fold = (fold_from + c * NBLD == fold_to).astype(jnp.float32).astype(jnp.bfloat16)
        folded = folded + jnp.dot(spread, fold, preferred_element_type=jnp.float32)
    rs_stage[...] = folded.astype(jnp.bfloat16).reshape(nz, FLOC * sloc, 128)

    rs_copies = []
    for r in range(1, nz):
        to = (z + r) % nz
        rs_copies.append(
            pltpu.make_async_remote_copy(
                src_ref=rs_stage.at[to], dst_ref=rs_recv.at[z], send_sem=rs_ssem.at[r], recv_sem=rs_rsem.at[r],
                device_id=(b, to), device_id_type=MESH,
            )
        )
        rs_copies[-1].start()
    rs_recv[z] = rs_stage[z]

    for q in range(nb):
        piece = pl.ds(q * bloc, bloc)
        label = lax.broadcasted_iota(jnp.int32, (2 * NBLD, bloc), 0) % NBLD
        sel_v[:, piece] = (label == owner_ref[:, piece]).astype(jnp.float32).astype(jnp.bfloat16)

    here = sel_v[0:NBLD, pl.ds(pl.multiple_of(b * bloc, 128), bloc)]
    width = 1024

    cross_copies = []

    def gather_away(d):
        pair_copies[d].wait()

        def step(i, carry):
            piece = pl.ds(pl.multiple_of(i * width, width), width)
            total = jnp.dot(here, pair_v[turns[0], d, :, piece], preferred_element_type=jnp.float32)
            cross_stage[d, :, piece] = total.astype(jnp.bfloat16)
            return carry

        lax.fori_loop(0, bores // width, step, 0)
        cross_copies.append(
            pltpu.make_async_remote_copy(
                src_ref=cross_stage.at[d], dst_ref=cross_recv.at[d], send_sem=cr_ssem.at[d], recv_sem=cr_rsem.at[d],
                device_id=(sibling, z), device_id_type=MESH,
            )
        )
        cross_copies[-1].start()

    def gather_here(d):
        pair_copies[2 + d].wait()
        cross_copies[d].wait_recv()

        def step(i, carry):
            piece = pl.ds(pl.multiple_of(i * width, width), width)
            total = jnp.dot(here, pair_v[turns[1], d, :, piece], preferred_element_type=jnp.float32)
            total = total + cross_recv[d, :, piece].astype(jnp.float32)
            grid_v[pl.ds(d * NBLD, NBLD), piece] = total.astype(jnp.bfloat16)
            return carry

        lax.fori_loop(0, bores // width, step, 0)

    gather_away(0)
    gather_away(1)

    for copy in rs_copies:
        copy.wait_recv()
    spec = rs_recv[0].astype(jnp.float32)
    for k in range(1, nz):
        spec = spec + rs_recv[k].astype(jnp.float32)
    bs_stage[...] = spec.astype(jnp.bfloat16).reshape(FLOC, sloc, 128)
    bs_all[b] = bs_stage[core]
    bs_copies = []
    for r in range(1, nb):
        to = (b + r) % nb
        bs_copies.append(
            pltpu.make_async_remote_copy(
                src_ref=bs_stage.at[to % 2], dst_ref=bs_all.at[b], send_sem=bs_ssem.at[r], recv_sem=bs_rsem.at[r],
                device_id=(to, z), device_id_type=MESH,
            )
        )
        bs_copies[-1].start()

    fw_copies = []
    for r in range(1, chips):
        share_copies[r - 1].wait_recv()
        origin = (chip + chips - r) % chips * 2 + core
        fw_copies.append(
            pltpu.make_async_remote_copy(
                src_ref=share_v.at[origin], dst_ref=share_v.at[origin], send_sem=fw_send.at[r], recv_sem=fw_recv.at[r],
                device_id=(sibling, z), device_id_type=MESH,
            )
        )
        fw_copies[-1].start()

    gather_here(0)
    gather_here(1)

    own_share.wait()
    share_copies[-1].wait_recv()
    for copy in fw_copies:
        copy.wait_recv()
    for copy in bs_copies:
        copy.wait_recv()

    spec_all = bs_all[...].reshape(scenarios, 128).astype(jnp.float32)
    half = lax.broadcasted_iota(jnp.int32, (scenarios, 128), 1) // NBLD
    spec_c = jnp.concatenate([jnp.where(half == c, spec_all, 0.0).astype(jnp.bfloat16) for c in range(2)], 0)

    def source_step(q, walls):
        piece = pl.ds(pl.multiple_of(q * bloc, 128), bloc)
        weight = share_v[q].astype(jnp.float32)
        picked = jnp.dot(spec_c, sel_v[:, piece], preferred_element_type=jnp.float32)
        source = (picked.reshape(2, scenarios, bloc) * weight).astype(jnp.bfloat16).reshape(2 * scenarios, bloc)
        return walls + lax.dot_general(source, grid_v[:, piece], NT, preferred_element_type=jnp.float32)

    walls = lax.fori_loop(0, nb, source_step, jnp.zeros((2 * scenarios, 128), jnp.float32), unroll=8)
    sign = jnp.where(lax.broadcasted_iota(jnp.int32, (scenarios, 128), 1) < NBLD, -1.0, 1.0)
    joined = (walls[:scenarios] + sign * pltpu.roll(walls[scenarios:], NBLD, 1)) * (NBLD / bores)
    wall_stage[...] = joined.reshape(nb * nz, s4, 128)

    slot = z * FLOC + core
    wl_copies = []
    for r, k in near_first[::-1]:
        to_b, to_z = (b + r) % nb, (z + k) % nz
        wl_copies.append(
            pltpu.make_async_remote_copy(
                src_ref=wall_stage.at[to_b * nz + to_z], dst_ref=wall_recv.at[slot, chip],
                send_sem=wl_ssem.at[r, k], recv_sem=wl_rsem.at[r, k],
                device_id=(to_b, to_z), device_id_type=MESH,
            )
        )
        wl_copies[-1].start()
    wall_recv[slot, chip] = wall_stage[b * nz + z]
    for copy in share_copies + rs_copies + bs_copies + fw_copies + cross_copies:
        copy.wait_send()
    for copy in wl_copies:
        copy.wait()
    wall = wall_recv[:, 0]
    for q in range(1, chips):
        wall = wall + wall_recv[:, q]
    out_ref[...] = wall.reshape(freqs * s4, 128)


def superpose(loads, pair_spectra, share, owners, freq_index, nb, nz):
    sloc, _, tloc = loads.shape
    bloc, bores = pair_spectra.shape[2:]
    scenarios = share.shape[0]
    freqs = freq_index.shape[0]
    s4 = sloc // nz
    bf16, f32, dma = jnp.bfloat16, jnp.float32, pltpu.SemaphoreType.DMA
    anywhere = pl.BlockSpec(memory_space=pl.ANY)
    return pl.pallas_call(
        functools.partial(superpose_kernel, nb, nz, tloc * nz),
        out_shape=pltpu.VMEM((nz * FLOC * s4, 128), f32),
        in_specs=[
            pl.BlockSpec(memory_space=pltpu.SMEM),
            pl.BlockSpec(memory_space=pltpu.VMEM),
            anywhere,
            anywhere,
            anywhere,
        ],
        out_specs=pl.BlockSpec(memory_space=pltpu.VMEM),
        scratch_shapes=[
            pltpu.VMEM(loads.shape, bf16),
            pltpu.VMEM(pair_spectra.shape, bf16),
            pltpu.VMEM((nb, scenarios, bloc), bf16),
            pltpu.VMEM((2 * NBLD, bores), bf16),
            pltpu.VMEM((2 * NBLD, bores), bf16),
            pltpu.VMEM((2, NBLD, bores), bf16),
            pltpu.VMEM((2, NBLD, bores), bf16),
            pltpu.VMEM((2 * freqs, sloc * NBLD), f32),
            pltpu.VMEM((nz, FLOC * sloc, 128), bf16),
            pltpu.VMEM((nz, FLOC * sloc, 128), bf16),
            pltpu.VMEM((FLOC, sloc, 128), bf16),
            pltpu.VMEM((nb, sloc, 128), bf16),
            pltpu.VMEM((nb * nz, s4, 128), f32),
            pltpu.VMEM((freqs, nb // 2, s4, 128), f32),
            dma((4,)),
            dma((FLOC, 2)),
            dma,
            dma((nb // 2,)),
            dma((nb // 2,)),
            dma((nb // 2,)),
            dma((nb // 2,)),
            dma((2,)),
            dma((2,)),
            dma((nz,)),
            dma((nz,)),
            dma((nb,)),
            dma((nb,)),
            dma((nb, nz)),
            dma((nb, nz)),
        ],
        compiler_params=pltpu.CompilerParams(
            collective_id=0, has_side_effects=True, vmem_limit_bytes=56 * 2**20
        ),
        name="superpose",
    )(freq_index, owners, loads, pair_spectra, share)


def inverse_kernel(hours, freq_ref, wall_v, out_hbm, out_v, out_sem):
    freqs = freq_ref.shape[0]
    s4 = out_hbm.shape[0]
    parts = out_sem.shape[0]
    count = hours // parts
    harmonics = harmonic_column(freq_ref, freqs)
    base_cos, base_sin = cos_sin(harmonics, 0, count, hours)
    turn_cos, turn_sin = cos_sin(harmonics, 0, 128, hours, count)
    low = lax.broadcasted_iota(jnp.int32, (freqs, 128), 1) < NBLD
    real, imag = [], []
    for s in range(0, s4, 2):
        one = wall_v[pl.ds(s, freqs, stride=s4), :]
        two = wall_v[pl.ds(s + 1, freqs, stride=s4), :]
        real.append(jnp.where(low, one, pltpu.roll(two, NBLD, 1)))
        imag.append(jnp.where(low, pltpu.roll(one, NBLD, 1), two))
    left = jnp.concatenate([jnp.concatenate(real, 1), -jnp.concatenate(imag, 1)], 0)
    upper, lower = halves(left * (1.0 / math.sqrt(freqs)))
    upper, lower = upper.astype(jnp.float32), lower.astype(jnp.float32)
    left = jnp.concatenate([upper, upper, lower], 0).T.astype(jnp.bfloat16)
    width = min(512, count)
    copies = []
    for i in range(parts):
        c, s = turn_cos[:, i : i + 1], turn_sin[:, i : i + 1]
        for j in range(0, count, width):
            piece = slice(j, j + width)
            cos = base_cos[:, piece] * c - base_sin[:, piece] * s
            sin = base_sin[:, piece] * c + base_cos[:, piece] * s
            upper, lower = halves(jnp.concatenate([cos, sin], 0))
            right = jnp.concatenate([upper, lower, upper], 0)
            total = jnp.dot(left, right, preferred_element_type=jnp.float32)
            out_v[:, :, pl.ds(i * count + j, width)] = total.astype(jnp.bfloat16).reshape(s4, NBLD, width)
        piece = pl.ds(i * count, count)
        copies.append(pltpu.make_async_copy(out_v.at[:, :, piece], out_hbm.at[:, :, piece], out_sem.at[i]))
        copies[-1].start()
    for copy in copies:
        copy.wait()


def inverse(freq_index, wall, s4, hours):
    parts = 8
    return pl.pallas_call(
        functools.partial(inverse_kernel, hours),
        out_shape=jax.ShapeDtypeStruct((s4, NBLD, hours), jnp.bfloat16),
        in_specs=[pl.BlockSpec(memory_space=pltpu.SMEM), pl.BlockSpec(memory_space=pltpu.VMEM)],
        out_specs=pl.BlockSpec(memory_space=pl.ANY),
        scratch_shapes=[
            pltpu.VMEM((s4, NBLD, hours), jnp.bfloat16),
            pltpu.SemaphoreType.DMA((parts,)),
        ],
        compiler_params=pltpu.CompilerParams(vmem_limit_bytes=56 * 2**20),
        name="inverse",
    )(freq_index, pltpu.with_memory_space_constraint(wall, pltpu.VMEM))


def solution(mesh):
    nb, nz = mesh.shape["bore"], mesh.shape["freq"]

    def body(loads, pair_spectra, share, assignment, freq_index):
        owners = assignment.reshape(1, -1)
        wall = superpose(loads, pair_spectra, share, owners, freq_index, nb, nz)
        return inverse(freq_index, wall, loads.shape[0] // nz, loads.shape[2] * nz)

    return jax.shard_map(
        body,
        mesh=mesh,
        in_specs=(
            P("bore", None, "freq"),
            P("freq", None, "bore", None),
            P(None, "bore"),
            P(),
            P(),
        ),
        out_specs=P(("bore", "freq"), None, None),
        check_vma=False,
    )
```

```python
import functools
import math

import jax
import jax.numpy as jnp
from jax import lax
from jax.experimental import pallas as pl
from jax.experimental.pallas import tpu as pltpu
from jax.sharding import PartitionSpec as P

NBLD = 64
FLOC = 2
MESH = pl.DeviceIdType.MESH
NT = (((1,), (1,)), ((), ()))
TN = (((0,), (0,)), ((), ()))


def harmonic_column(freq_ref, freqs):
    row = lax.broadcasted_iota(jnp.int32, (freqs, 1), 0)
    column = jnp.zeros((freqs, 1), jnp.int32)
    for k in range(freqs):
        column = jnp.where(row == k, freq_ref[k], column)
    return column


def cos_sin(harmonics, first_hour, count, hours, stride=1):
    freqs = harmonics.shape[0]
    t = lax.broadcasted_iota(jnp.int32, (freqs, count), 1) * stride + first_hour
    phase = (harmonics * t) & (hours - 1)
    quarter = hours // 4
    turn = (phase + quarter // 2) // quarter
    x = (phase - turn * quarter).astype(jnp.float32) * (2.0 * math.pi / hours)
    y = x * x
    c = 1.0 + y * (-0.5 + y * (1 / 24 + y * (-1 / 720 + y * (1 / 40320 - y * (1 / 3628800)))))
    s = x * (1.0 + y * (-1 / 6 + y * (1 / 120 + y * (-1 / 5040 + y * (1 / 362880)))))
    odd = (turn & 1) == 1
    cos = jnp.where(odd, s, c)
    sin = jnp.where(odd, c, s)
    cos = jnp.where((turn == 1) | (turn == 2), -cos, cos)
    sin = jnp.where((turn == 2) | (turn == 3), -sin, sin)
    return cos, sin


def halves(x):
    upper = x.astype(jnp.bfloat16)
    return upper, (x - upper.astype(jnp.float32)).astype(jnp.bfloat16)


def superpose_kernel(
    nb, nz, hours, freq_ref, owner_ref, loads_hbm, pair_hbm, share_hbm, out_ref,
    loads_v, pair_v, share_v, sel_v, grid_v, cross_stage, cross_recv,
    rs_stage, rs_recv, bs_stage, bs_all, wall_stage, wall_recv,
    loads_sem, pair_sem, own_sem, sh_send, sh_recv, fw_send, fw_recv,
    cr_ssem, cr_rsem, rs_ssem, rs_rsem, bs_ssem, bs_rsem, wl_ssem, wl_rsem,
):
    b = lax.axis_index("bore")
    z = lax.axis_index("freq")
    sloc = loads_hbm.shape[0]
    tloc = loads_hbm.shape[2]
    freqs = freq_ref.shape[0]
    bores = owner_ref.shape[1]
    bloc = pair_hbm.shape[2]
    scenarios = share_hbm.shape[0]
    s4 = sloc // nz
    core = b % 2
    chip = b // 2
    chips = nb // 2
    sibling = b + 1 - 2 * core
    near_first = sorted(
        ((r, k) for r in range(nb) for k in range(nz) if r or k), key=lambda rk: min(rk[1], nz - rk[1])
    )

    barrier = pltpu.get_barrier_semaphore()
    for r, k in near_first:
        pl.semaphore_signal(barrier, inc=1, device_id=((b + r) % nb, (z + k) % nz), device_id_type=MESH)

    sp = sloc // 2
    hp = tloc // 2
    load_copies = [
        [
            pltpu.make_async_copy(
                loads_hbm.at[pl.ds(i * sp, sp), :, pl.ds(h * hp, hp)],
                loads_v.at[pl.ds(i * sp, sp), :, pl.ds(h * hp, hp)],
                loads_sem.at[i, h],
            )
            for h in range(2)
        ]
        for i in range(2)
    ]
    for copy in load_copies[0] + load_copies[1]:
        copy.start()
    own_share = pltpu.make_async_copy(share_hbm, share_v.at[b], own_sem)
    own_share.start()
    turns = (1 - core, core)
    pair_copies = [
        pltpu.make_async_copy(pair_hbm.at[turns[i], d], pair_v.at[turns[i], d], pair_sem.at[i, d])
        for i in range(FLOC)
        for d in range(2)
    ]

    cos, sin = cos_sin(harmonic_column(freq_ref, freqs), z * tloc, tloc, hours)
    table = jnp.concatenate([*halves(cos), *halves(sin)], 0)
    lanes = sp * NBLD
    keep = lax.broadcasted_iota(jnp.int32, (sp, lanes), 1) // NBLD == lax.broadcasted_iota(jnp.int32, (sp, lanes), 0)
    fold_from = lax.broadcasted_iota(jnp.int32, (lanes, 128), 0) % NBLD
    fold_to = lax.broadcasted_iota(jnp.int32, (lanes, 128), 1)
    folds = [(fold_from + c * NBLD == fold_to).astype(jnp.float32).astype(jnp.bfloat16) for c in range(2)]

    pl.semaphore_wait(barrier, nb * nz - 1)

    share_copies = []
    for r in range(1, chips):
        share_copies.append(
            pltpu.make_async_remote_copy(
                src_ref=share_hbm, dst_ref=share_v.at[b], send_sem=sh_send.at[r], recv_sem=sh_recv.at[r],
                device_id=((chip + r) % chips * 2 + core, z), device_id_type=MESH,
            )
        )
    share_copies.append(
        pltpu.make_async_remote_copy(
            src_ref=share_hbm, dst_ref=share_v.at[b], send_sem=sh_send.at[0], recv_sem=sh_recv.at[0],
            device_id=(sibling, z), device_id_type=MESH,
        )
    )
    for copy in share_copies:
        copy.start()

    folded = []
    for i in range(2):
        spec = jnp.zeros((4 * freqs, lanes), jnp.float32)
        for h in range(2):
            load_copies[i][h].wait()
            pair_copies[2 * i + h].start()
            chunk = loads_v[pl.ds(i * sp, sp), :, pl.ds(h * hp, hp)].reshape(lanes, hp)
            spec = spec + lax.dot_general(
                table[:, h * hp : (h + 1) * hp], chunk, NT, preferred_element_type=jnp.float32
            )
        total = jnp.zeros((freqs * sp, 128), jnp.float32)
        for c in range(2):
            upper, lower = spec[2 * c * freqs : (2 * c + 1) * freqs], spec[(2 * c + 1) * freqs : (2 * c + 2) * freqs]
            part = (upper + lower) * ((1.0 - 2.0 * c) / math.sqrt(hours))
            spread = jnp.concatenate(
                [jnp.where(keep, part[k : k + 1], 0.0).astype(jnp.bfloat16) for k in range(freqs)], 0
            )
            total = total + jnp.dot(spread, folds[c], preferred_element_type=jnp.float32)
        folded.append(total.reshape(freqs, sp, 128))
    rs_stage[...] = jnp.concatenate(folded, 1).astype(jnp.bfloat16).reshape(nz, FLOC * sloc, 128)

    rs_copies = []
    for r in range(1, nz):
        to = (z + r) % nz
        rs_copies.append(
            pltpu.make_async_remote_copy(
                src_ref=rs_stage.at[to], dst_ref=rs_recv.at[z], send_sem=rs_ssem.at[r], recv_sem=rs_rsem.at[r],
                device_id=(b, to), device_id_type=MESH,
            )
        )
        rs_copies[-1].start()
    rs_recv[z] = rs_stage[z]

    for q in range(nb):
        piece = pl.ds(q * bloc, bloc)
        label = lax.broadcasted_iota(jnp.int32, (2 * NBLD, bloc), 0) % NBLD
        sel_v[:, piece] = (label == owner_ref[:, piece]).astype(jnp.float32).astype(jnp.bfloat16)

    here = sel_v[0:NBLD, pl.ds(pl.multiple_of(b * bloc, 128), bloc)]
    width = 1024

    cross_copies = []

    def gather_away(d):
        pair_copies[d].wait()

        def step(i, carry):
            piece = pl.ds(pl.multiple_of(i * width, width), width)
            total = jnp.dot(here, pair_v[turns[0], d, :, piece], preferred_element_type=jnp.float32)
            cross_stage[d, :, piece] = total.astype(jnp.bfloat16)
            return carry

        lax.fori_loop(0, bores // width, step, 0)
        cross_copies.append(
            pltpu.make_async_remote_copy(
                src_ref=cross_stage.at[d], dst_ref=cross_recv.at[d], send_sem=cr_ssem.at[d], recv_sem=cr_rsem.at[d],
                device_id=(sibling, z), device_id_type=MESH,
            )
        )
        cross_copies[-1].start()

    def gather_here(d):
        pair_copies[2 + d].wait()
        cross_copies[d].wait_recv()

        def step(i, carry):
            piece = pl.ds(pl.multiple_of(i * width, width), width)
            total = jnp.dot(here, pair_v[turns[1], d, :, piece], preferred_element_type=jnp.float32)
            total = total + cross_recv[d, :, piece].astype(jnp.float32)
            grid_v[pl.ds(d * NBLD, NBLD), piece] = total.astype(jnp.bfloat16)
            return carry

        lax.fori_loop(0, bores // width, step, 0)

    gather_away(0)
    gather_away(1)

    for copy in rs_copies:
        copy.wait_recv()
    spec = rs_recv[0].astype(jnp.float32)
    for k in range(1, nz):
        spec = spec + rs_recv[k].astype(jnp.float32)
    bs_stage[...] = spec.astype(jnp.bfloat16).reshape(FLOC, sloc, 128)
    bs_all[b] = bs_stage[core]
    bs_copies = []
    for r in range(1, nb):
        to = (b + r) % nb
        bs_copies.append(
            pltpu.make_async_remote_copy(
                src_ref=bs_stage.at[to % 2], dst_ref=bs_all.at[b], send_sem=bs_ssem.at[r], recv_sem=bs_rsem.at[r],
                device_id=(to, z), device_id_type=MESH,
            )
        )
        bs_copies[-1].start()

    fw_copies = []
    for r in range(1, chips):
        share_copies[r - 1].wait_recv()
        origin = (chip + chips - r) % chips * 2 + core
        fw_copies.append(
            pltpu.make_async_remote_copy(
                src_ref=share_v.at[origin], dst_ref=share_v.at[origin], send_sem=fw_send.at[r], recv_sem=fw_recv.at[r],
                device_id=(sibling, z), device_id_type=MESH,
            )
        )
        fw_copies[-1].start()

    gather_here(0)
    gather_here(1)

    own_share.wait()
    share_copies[-1].wait_recv()
    for copy in fw_copies:
        copy.wait_recv()
    for copy in bs_copies:
        copy.wait_recv()

    spec_all = bs_all[...].reshape(scenarios, 128).astype(jnp.float32)
    half = lax.broadcasted_iota(jnp.int32, (scenarios, 128), 1) // NBLD
    spec_c = jnp.concatenate([jnp.where(half == c, spec_all, 0.0).astype(jnp.bfloat16) for c in range(2)], 0)

    def source_step(q, walls):
        piece = pl.ds(pl.multiple_of(q * bloc, 128), bloc)
        weight = share_v[q].astype(jnp.float32)
        picked = jnp.dot(spec_c, sel_v[:, piece], preferred_element_type=jnp.float32)
        source = (picked.reshape(2, scenarios, bloc) * weight).astype(jnp.bfloat16).reshape(2 * scenarios, bloc)
        return walls + lax.dot_general(source, grid_v[:, piece], NT, preferred_element_type=jnp.float32)

    walls = lax.fori_loop(0, nb, source_step, jnp.zeros((2 * scenarios, 128), jnp.float32), unroll=8)
    sign = jnp.where(lax.broadcasted_iota(jnp.int32, (scenarios, 128), 1) < NBLD, -1.0, 1.0)
    joined = (walls[:scenarios] + sign * pltpu.roll(walls[scenarios:], NBLD, 1)) * (NBLD / bores)
    wall_stage[...] = joined.reshape(nb * nz, s4, 128)

    slot = z * FLOC + core
    wl_copies = []
    for r, k in near_first[::-1]:
        to_b, to_z = (b + r) % nb, (z + k) % nz
        wl_copies.append(
            pltpu.make_async_remote_copy(
                src_ref=wall_stage.at[to_b * nz + to_z], dst_ref=wall_recv.at[slot, chip],
                send_sem=wl_ssem.at[r, k], recv_sem=wl_rsem.at[r, k],
                device_id=(to_b, to_z), device_id_type=MESH,
            )
        )
        wl_copies[-1].start()
    wall_recv[slot, chip] = wall_stage[b * nz + z]
    for copy in share_copies + rs_copies + bs_copies + fw_copies + cross_copies:
        copy.wait_send()
    for copy in wl_copies:
        copy.wait()
    wall = wall_recv[:, 0]
    for q in range(1, chips):
        wall = wall + wall_recv[:, q]
    out_ref[...] = wall.reshape(freqs * s4, 128)


def superpose(loads, pair_spectra, share, owners, freq_index, nb, nz):
    sloc, _, tloc = loads.shape
    bloc, bores = pair_spectra.shape[2:]
    scenarios = share.shape[0]
    freqs = freq_index.shape[0]
    s4 = sloc // nz
    bf16, f32, dma = jnp.bfloat16, jnp.float32, pltpu.SemaphoreType.DMA
    anywhere = pl.BlockSpec(memory_space=pl.ANY)
    return pl.pallas_call(
        functools.partial(superpose_kernel, nb, nz, tloc * nz),
        out_shape=pltpu.VMEM((nz * FLOC * s4, 128), f32),
        in_specs=[
            pl.BlockSpec(memory_space=pltpu.SMEM),
            pl.BlockSpec(memory_space=pltpu.VMEM),
            anywhere,
            anywhere,
            anywhere,
        ],
        out_specs=pl.BlockSpec(memory_space=pltpu.VMEM),
        scratch_shapes=[
            pltpu.VMEM(loads.shape, bf16),
            pltpu.VMEM(pair_spectra.shape, bf16),
            pltpu.VMEM((nb, scenarios, bloc), bf16),
            pltpu.VMEM((2 * NBLD, bores), bf16),
            pltpu.VMEM((2 * NBLD, bores), bf16),
            pltpu.VMEM((2, NBLD, bores), bf16),
            pltpu.VMEM((2, NBLD, bores), bf16),
            pltpu.VMEM((nz, FLOC * sloc, 128), bf16),
            pltpu.VMEM((nz, FLOC * sloc, 128), bf16),
            pltpu.VMEM((FLOC, sloc, 128), bf16),
            pltpu.VMEM((nb, sloc, 128), bf16),
            pltpu.VMEM((nb * nz, s4, 128), f32),
            pltpu.VMEM((freqs, nb // 2, s4, 128), f32),
            dma((2, 2)),
            dma((FLOC, 2)),
            dma,
            dma((nb // 2,)),
            dma((nb // 2,)),
            dma((nb // 2,)),
            dma((nb // 2,)),
            dma((2,)),
            dma((2,)),
            dma((nz,)),
            dma((nz,)),
            dma((nb,)),
            dma((nb,)),
            dma((nb, nz)),
            dma((nb, nz)),
        ],
        compiler_params=pltpu.CompilerParams(
            collective_id=0, has_side_effects=True, vmem_limit_bytes=56 * 2**20
        ),
        name="superpose",
    )(freq_index, owners, loads, pair_spectra, share)


def inverse_kernel(hours, freq_ref, wall_v, out_hbm, out_v, out_sem):
    freqs = freq_ref.shape[0]
    s4 = out_hbm.shape[0]
    parts = out_sem.shape[0]
    count = hours // parts
    harmonics = harmonic_column(freq_ref, freqs)
    base_cos, base_sin = cos_sin(harmonics, 0, count, hours)
    turn_cos, turn_sin = cos_sin(harmonics, 0, 128, hours, count)
    low = lax.broadcasted_iota(jnp.int32, (freqs, 128), 1) < NBLD
    real, imag = [], []
    for s in range(0, s4, 2):
        one = wall_v[pl.ds(s, freqs, stride=s4), :]
        two = wall_v[pl.ds(s + 1, freqs, stride=s4), :]
        real.append(jnp.where(low, one, pltpu.roll(two, NBLD, 1)))
        imag.append(jnp.where(low, pltpu.roll(one, NBLD, 1), two))
    left = jnp.concatenate([jnp.concatenate(real, 1), -jnp.concatenate(imag, 1)], 0)
    upper, lower = halves(left * (1.0 / math.sqrt(freqs)))
    upper, lower = upper.astype(jnp.float32), lower.astype(jnp.float32)
    left = jnp.concatenate([upper, upper, lower], 0).T.astype(jnp.bfloat16)
    width = min(512, count)
    copies = []
    for i in range(parts):
        c, s = turn_cos[:, i : i + 1], turn_sin[:, i : i + 1]
        for j in range(0, count, width):
            piece = slice(j, j + width)
            cos = base_cos[:, piece] * c - base_sin[:, piece] * s
            sin = base_sin[:, piece] * c + base_cos[:, piece] * s
            upper, lower = halves(jnp.concatenate([cos, sin], 0))
            right = jnp.concatenate([upper, lower, upper], 0)
            total = jnp.dot(left, right, preferred_element_type=jnp.float32)
            out_v[:, :, pl.ds(i * count + j, width)] = total.astype(jnp.bfloat16).reshape(s4, NBLD, width)
        piece = pl.ds(i * count, count)
        copies.append(pltpu.make_async_copy(out_v.at[:, :, piece], out_hbm.at[:, :, piece], out_sem.at[i]))
        copies[-1].start()
    for copy in copies:
        copy.wait()


def inverse(freq_index, wall, s4, hours):
    parts = 8
    return pl.pallas_call(
        functools.partial(inverse_kernel, hours),
        out_shape=jax.ShapeDtypeStruct((s4, NBLD, hours), jnp.bfloat16),
        in_specs=[pl.BlockSpec(memory_space=pltpu.SMEM), pl.BlockSpec(memory_space=pltpu.VMEM)],
        out_specs=pl.BlockSpec(memory_space=pl.ANY),
        scratch_shapes=[
            pltpu.VMEM((s4, NBLD, hours), jnp.bfloat16),
            pltpu.SemaphoreType.DMA((parts,)),
        ],
        compiler_params=pltpu.CompilerParams(vmem_limit_bytes=56 * 2**20),
        name="inverse",
    )(freq_index, pltpu.with_memory_space_constraint(wall, pltpu.VMEM))


def solution(mesh):
    nb, nz = mesh.shape["bore"], mesh.shape["freq"]

    def body(loads, pair_spectra, share, assignment, freq_index):
        owners = assignment.reshape(1, -1)
        wall = superpose(loads, pair_spectra, share, owners, freq_index, nb, nz)
        return inverse(freq_index, wall, loads.shape[0] // nz, loads.shape[2] * nz)

    return jax.shard_map(
        body,
        mesh=mesh,
        in_specs=(
            P("bore", None, "freq"),
            P("freq", None, "bore", None),
            P(None, "bore"),
            P(),
            P(),
        ),
        out_specs=P(("bore", "freq"), None, None),
        check_vma=False,
    )
```

```python
import functools
import math

import jax
import jax.numpy as jnp
from jax import lax
from jax.experimental import pallas as pl
from jax.experimental.pallas import tpu as pltpu
from jax.sharding import PartitionSpec as P

NBLD = 64
FLOC = 2
MESH = pl.DeviceIdType.MESH
NT = (((1,), (1,)), ((), ()))
TN = (((0,), (0,)), ((), ()))


def harmonic_column(freq_ref, freqs):
    row = lax.broadcasted_iota(jnp.int32, (freqs, 1), 0)
    column = jnp.zeros((freqs, 1), jnp.int32)
    for k in range(freqs):
        column = jnp.where(row == k, freq_ref[k], column)
    return column


def cos_sin(harmonics, first_hour, count, hours, stride=1):
    freqs = harmonics.shape[0]
    t = lax.broadcasted_iota(jnp.int32, (freqs, count), 1) * stride + first_hour
    phase = (harmonics * t) & (hours - 1)
    quarter = hours // 4
    turn = (phase + quarter // 2) // quarter
    x = (phase - turn * quarter).astype(jnp.float32) * (2.0 * math.pi / hours)
    y = x * x
    c = 1.0 + y * (-0.5 + y * (1 / 24 + y * (-1 / 720 + y * (1 / 40320 - y * (1 / 3628800)))))
    s = x * (1.0 + y * (-1 / 6 + y * (1 / 120 + y * (-1 / 5040 + y * (1 / 362880)))))
    odd = (turn & 1) == 1
    cos = jnp.where(odd, s, c)
    sin = jnp.where(odd, c, s)
    cos = jnp.where((turn == 1) | (turn == 2), -cos, cos)
    sin = jnp.where((turn == 2) | (turn == 3), -sin, sin)
    return cos, sin


def halves(x):
    upper = x.astype(jnp.bfloat16)
    return upper, (x - upper.astype(jnp.float32)).astype(jnp.bfloat16)


def superpose_kernel(
    nb, nz, hours, freq_ref, owner_ref, loads_hbm, pair_hbm, share_hbm, out_ref,
    loads_v, pair_v, share_v, sel_v, grid_v, cross_stage, cross_recv,
    bs_stage, bs_all, wall_stage, wall_recv,
    loads_sem, pair_sem, own_sem, sh_send, sh_recv, fw_send, fw_recv,
    cr_ssem, cr_rsem, bs_ssem, bs_rsem, wl_ssem, wl_rsem,
):
    b = lax.axis_index("bore")
    z = lax.axis_index("freq")
    sloc = loads_hbm.shape[0]
    tloc = loads_hbm.shape[2]
    freqs = freq_ref.shape[0]
    bores = owner_ref.shape[1]
    bloc = pair_hbm.shape[2]
    scenarios = share_hbm.shape[0]
    s4 = sloc // nz
    core = b % 2
    chip = b // 2
    chips = nb // 2
    sibling = b + 1 - 2 * core
    near_first = sorted(
        ((r, k) for r in range(nb) for k in range(nz) if r or k), key=lambda rk: min(rk[1], nz - rk[1])
    )

    own_share = pltpu.make_async_copy(share_hbm, share_v.at[b], own_sem)
    own_share.start()
    sp = sloc // 2
    hp = tloc // 2
    load_copies = [
        [
            pltpu.make_async_copy(
                loads_hbm.at[pl.ds(i * sp, sp), :, pl.ds(h * hp, hp)],
                loads_v.at[pl.ds(i * sp, sp), :, pl.ds(h * hp, hp)],
                loads_sem.at[i, h],
            )
            for h in range(2)
        ]
        for i in range(2)
    ]
    for copy in load_copies[0] + load_copies[1]:
        copy.start()
    barrier = pltpu.get_barrier_semaphore()
    for r, k in near_first:
        pl.semaphore_signal(barrier, inc=1, device_id=((b + r) % nb, (z + k) % nz), device_id_type=MESH)

    turns = (1 - core, core)
    pair_copies = [
        pltpu.make_async_copy(pair_hbm.at[turns[i], d], pair_v.at[turns[i], d], pair_sem.at[i, d])
        for i in range(FLOC)
        for d in range(2)
    ]

    cos, sin = cos_sin(harmonic_column(freq_ref, freqs), z * tloc, tloc, hours)
    table = jnp.concatenate([*halves(cos), *halves(sin)], 0)
    lanes = sp * NBLD
    keep = lax.broadcasted_iota(jnp.int32, (sp, lanes), 1) // NBLD == lax.broadcasted_iota(jnp.int32, (sp, lanes), 0)
    fold_from = lax.broadcasted_iota(jnp.int32, (lanes, 128), 0) % NBLD
    fold_to = lax.broadcasted_iota(jnp.int32, (lanes, 128), 1)
    folds = [(fold_from + c * NBLD == fold_to).astype(jnp.float32).astype(jnp.bfloat16) for c in range(2)]

    square = chips == 4
    over_x = chip + 1 - 2 * (chip % 2)
    over_y = (chip + 2) % chips
    first_hops = (over_x, over_y) if square else tuple((chip + r) % chips for r in range(1, chips))
    first_from = first_hops if square else tuple((chip + chips - r) % chips for r in range(1, chips))
    share_copies = [
        pltpu.make_async_remote_copy(
            src_ref=share_v.at[b], dst_ref=share_v.at[b], send_sem=sh_send.at[r], recv_sem=sh_recv.at[r],
            device_id=device, device_id_type=MESH,
        )
        for r, device in enumerate([(to * 2 + core, z) for to in first_hops] + [(sibling, z)])
    ]

    for q in range(nb):
        piece = pl.ds(q * bloc, bloc)
        label = lax.broadcasted_iota(jnp.int32, (2 * NBLD, bloc), 0) % NBLD
        sel_v[:, piece] = (label == owner_ref[:, piece]).astype(jnp.float32).astype(jnp.bfloat16)

    pl.semaphore_wait(barrier, nb * nz - 1)
    own_share.wait()
    for copy in share_copies:
        copy.start()

    folded = []
    for i in range(2):
        spec = jnp.zeros((4 * freqs, lanes), jnp.float32)
        for h in range(2):
            load_copies[i][h].wait()
            pair_copies[2 * i + h].start()
            chunk = loads_v[pl.ds(i * sp, sp), :, pl.ds(h * hp, hp)].reshape(lanes, hp)
            spec = spec + lax.dot_general(
                table[:, h * hp : (h + 1) * hp], chunk, NT, preferred_element_type=jnp.float32
            )
        total = jnp.zeros((freqs * sp, 128), jnp.float32)
        for c in range(2):
            upper, lower = spec[2 * c * freqs : (2 * c + 1) * freqs], spec[(2 * c + 1) * freqs : (2 * c + 2) * freqs]
            part = (upper + lower) * ((1.0 - 2.0 * c) / math.sqrt(hours))
            spread = jnp.concatenate(
                [jnp.where(keep, part[k : k + 1], 0.0).astype(jnp.bfloat16) for k in range(freqs)], 0
            )
            total = total + jnp.dot(spread, folds[c], preferred_element_type=jnp.float32)
        folded.append(total.reshape(freqs, sp, 128))
    bs_stage[...] = jnp.concatenate(folded, 1).astype(jnp.bfloat16)

    bs_copies = []
    for r, k in near_first[::-1]:
        to_b, to_z = (b + r) % nb, (z + k) % nz
        bs_copies.append(
            pltpu.make_async_remote_copy(
                src_ref=bs_stage.at[to_z * FLOC + to_b % 2], dst_ref=bs_all.at[z, b],
                send_sem=bs_ssem.at[r, k], recv_sem=bs_rsem.at[r, k],
                device_id=(to_b, to_z), device_id_type=MESH,
            )
        )
        bs_copies[-1].start()
    bs_all[z, b] = bs_stage[z * FLOC + core]

    fw_copies = []

    def forward(r, origin, rows, device):
        there = share_v.at[origin, rows]
        fw_copies.append(
            pltpu.make_async_remote_copy(
                src_ref=there, dst_ref=there, send_sem=fw_send.at[r], recv_sem=fw_recv.at[r],
                device_id=(device, z), device_id_type=MESH,
            )
        )
        fw_copies[-1].start()

    here = sel_v[0:NBLD, pl.ds(pl.multiple_of(b * bloc, 128), bloc)]
    width = 2048

    cross_copies = []

    def gather_away(d):
        pair_copies[d].wait()

        def step(i, carry):
            piece = pl.ds(pl.multiple_of(i * width, width), width)
            total = jnp.dot(here, pair_v[turns[0], d, :, piece], preferred_element_type=jnp.float32)
            cross_stage[d, :, piece] = total.astype(jnp.bfloat16)
            return carry

        lax.fori_loop(0, bores // width, step, 0)
        cross_copies.append(
            pltpu.make_async_remote_copy(
                src_ref=cross_stage.at[d], dst_ref=cross_recv.at[d], send_sem=cr_ssem.at[d], recv_sem=cr_rsem.at[d],
                device_id=(sibling, z), device_id_type=MESH,
            )
        )
        cross_copies[-1].start()

    def gather_here(d):
        pair_copies[2 + d].wait()
        cross_copies[d].wait_recv()

        def step(i, carry):
            piece = pl.ds(pl.multiple_of(i * width, width), width)
            total = jnp.dot(here, pair_v[turns[1], d, :, piece], preferred_element_type=jnp.float32)
            total = total + cross_recv[d, :, piece].astype(jnp.float32)
            grid_v[pl.ds(d * NBLD, NBLD), piece] = total.astype(jnp.bfloat16)
            return carry

        lax.fori_loop(0, bores // width, step, 0)

    gather_away(0)
    gather_away(1)

    every = slice(0, scenarios)
    for r, origin in enumerate(first_from):
        share_copies[r].wait_recv()
        if square:
            rows = pl.ds(r * (scenarios // 2), scenarios // 2)
            forward(chips + r, origin * 2 + core, rows, first_hops[1 - r] * 2 + core)
        forward(r, origin * 2 + core, every, sibling)


    gather_here(0)
    gather_here(1)

    if square:
        for r in range(2):
            fw_copies[2 * r].wait_recv()
        forward(2, (over_x + 2) % chips * 2 + core, every, sibling)

    share_copies[-1].wait_recv()
    for copy in (fw_copies[1], fw_copies[3]) if square else fw_copies:
        copy.wait_recv()
    for copy in bs_copies:
        copy.wait_recv()

    spec_all = bs_all[0].astype(jnp.float32)
    for k in range(1, nz):
        spec_all = spec_all + bs_all[k].astype(jnp.float32)
    spec_all = spec_all.reshape(scenarios, 128)
    half = lax.broadcasted_iota(jnp.int32, (scenarios, 128), 1) // NBLD
    spec_c = jnp.concatenate([jnp.where(half == c, spec_all, 0.0).astype(jnp.bfloat16) for c in range(2)], 0)

    def source_blocks(origins, walls):
        for q in origins:
            piece = pl.ds(pl.multiple_of(q * bloc, 128), bloc)
            weight = share_v[q].astype(jnp.float32)
            picked = jnp.dot(spec_c, sel_v[:, piece], preferred_element_type=jnp.float32)
            source = (picked.reshape(2, scenarios, bloc) * weight).astype(jnp.bfloat16).reshape(2 * scenarios, bloc)
            walls = walls + lax.dot_general(source, grid_v[:, piece], NT, preferred_element_type=jnp.float32)
        return walls

    walls = jnp.zeros((2 * scenarios, 128), jnp.float32)
    if square:
        walls = source_blocks([q * 2 + c for q in (chip, over_x, over_y) for c in range(2)], walls)
        fw_copies[4].wait_recv()
        diagonal = (over_x + 2) % chips
        walls = source_blocks([diagonal * 2 + c for c in range(2)], walls)
    else:
        walls = source_blocks(range(nb), walls)
    sign = jnp.where(lax.broadcasted_iota(jnp.int32, (scenarios, 128), 1) < NBLD, -1.0, 1.0)
    joined = (walls[:scenarios] + sign * pltpu.roll(walls[scenarios:], NBLD, 1)) * (NBLD / bores)
    wall_stage[...] = joined.reshape(nb * nz, s4, 128)

    slot = z * FLOC + core
    def wall_copy(r, to_z, from_z):
        to_b = (b + r) % nb
        return pltpu.make_async_remote_copy(
            src_ref=wall_stage.at[to_b * nz + to_z], dst_ref=wall_recv.at[slot, chip],
            send_sem=wl_ssem.at[r, to_z], recv_sem=wl_rsem.at[r, from_z],
            device_id=(to_b, to_z), device_id_type=MESH,
        )

    plane_first = []
    for k in range(nz):
        plane_first += [(r, k) for r in range(1, nb)]
        if k < nz - 1:
            plane_first.append((0, k + (z <= k).astype(jnp.int32)))
    for r, k in plane_first:
        wall_copy(r, k, z).start()
    wall_recv[slot, chip] = wall_stage[b * nz + z]
    for copy in share_copies + bs_copies + fw_copies + cross_copies:
        copy.wait_send()
    for r, k in plane_first:
        wall_copy(r, k, k).wait()
    wall = wall_recv[:, 0]
    for q in range(1, chips):
        wall = wall + wall_recv[:, q]
    out_ref[...] = wall.reshape(freqs * s4, 128)


def superpose(loads, pair_spectra, share, owners, freq_index, nb, nz):
    sloc, _, tloc = loads.shape
    bloc, bores = pair_spectra.shape[2:]
    scenarios = share.shape[0]
    freqs = freq_index.shape[0]
    s4 = sloc // nz
    bf16, f32, dma = jnp.bfloat16, jnp.float32, pltpu.SemaphoreType.DMA
    anywhere = pl.BlockSpec(memory_space=pl.ANY)
    return pl.pallas_call(
        functools.partial(superpose_kernel, nb, nz, tloc * nz),
        out_shape=pltpu.VMEM((nz * FLOC * s4, 128), f32),
        in_specs=[
            pl.BlockSpec(memory_space=pltpu.SMEM),
            pl.BlockSpec(memory_space=pltpu.VMEM),
            anywhere,
            anywhere,
            anywhere,
        ],
        out_specs=pl.BlockSpec(memory_space=pltpu.VMEM),
        scratch_shapes=[
            pltpu.VMEM(loads.shape, bf16),
            pltpu.VMEM(pair_spectra.shape, bf16),
            pltpu.VMEM((nb, scenarios, bloc), bf16),
            pltpu.VMEM((2 * NBLD, bores), bf16),
            pltpu.VMEM((2 * NBLD, bores), bf16),
            pltpu.VMEM((2, NBLD, bores), bf16),
            pltpu.VMEM((2, NBLD, bores), bf16),
            pltpu.VMEM((freqs, sloc, 128), bf16),
            pltpu.VMEM((nz, nb, sloc, 128), bf16),
            pltpu.VMEM((nb * nz, s4, 128), f32),
            pltpu.VMEM((freqs, nb // 2, s4, 128), f32),
            dma((2, 2)),
            dma((FLOC, 2)),
            dma,
            dma((nb // 2,)),
            dma((nb // 2,)),
            dma((nb // 2 + 2,)),
            dma((nb // 2 + 2,)),
            dma((2,)),
            dma((2,)),
            dma((nb, nz)),
            dma((nb, nz)),
            dma((nb, nz)),
            dma((nb, nz)),
        ],
        compiler_params=pltpu.CompilerParams(
            collective_id=0, has_side_effects=True, vmem_limit_bytes=56 * 2**20
        ),
        name="superpose",
    )(freq_index, owners, loads, pair_spectra, share)


def inverse_kernel(hours, freq_ref, wall_v, out_hbm, out_v, out_sem):
    freqs = freq_ref.shape[0]
    s4 = out_hbm.shape[0]
    parts = out_sem.shape[0]
    count = hours // parts
    harmonics = harmonic_column(freq_ref, freqs)
    base_cos, base_sin = cos_sin(harmonics, 0, count, hours)
    turn_cos, turn_sin = cos_sin(harmonics, 0, 128, hours, count)
    low = lax.broadcasted_iota(jnp.int32, (freqs, 128), 1) < NBLD
    real, imag = [], []
    for s in range(0, s4, 2):
        one = wall_v[pl.ds(s, freqs, stride=s4), :]
        two = wall_v[pl.ds(s + 1, freqs, stride=s4), :]
        real.append(jnp.where(low, one, pltpu.roll(two, NBLD, 1)))
        imag.append(jnp.where(low, pltpu.roll(one, NBLD, 1), two))
    left = jnp.concatenate([jnp.concatenate(real, 1), -jnp.concatenate(imag, 1)], 0)
    upper, lower = halves(left * (1.0 / math.sqrt(freqs)))
    upper, lower = upper.astype(jnp.float32), lower.astype(jnp.float32)
    left = jnp.concatenate([upper, upper, lower], 0).T.astype(jnp.bfloat16)
    width = min(512, count)
    copies = []
    for i in range(parts):
        c, s = turn_cos[:, i : i + 1], turn_sin[:, i : i + 1]
        for j in range(0, count, width):
            piece = slice(j, j + width)
            cos = base_cos[:, piece] * c - base_sin[:, piece] * s
            sin = base_sin[:, piece] * c + base_cos[:, piece] * s
            upper, lower = halves(jnp.concatenate([cos, sin], 0))
            right = jnp.concatenate([upper, lower, upper], 0)
            total = jnp.dot(left, right, preferred_element_type=jnp.float32)
            out_v[:, :, pl.ds(i * count + j, width)] = total.astype(jnp.bfloat16).reshape(s4, NBLD, width)
        piece = pl.ds(i * count, count)
        copies.append(pltpu.make_async_copy(out_v.at[:, :, piece], out_hbm.at[:, :, piece], out_sem.at[i]))
        copies[-1].start()
    for copy in copies:
        copy.wait()


def inverse(freq_index, wall, s4, hours):
    parts = 8
    return pl.pallas_call(
        functools.partial(inverse_kernel, hours),
        out_shape=jax.ShapeDtypeStruct((s4, NBLD, hours), jnp.bfloat16),
        in_specs=[pl.BlockSpec(memory_space=pltpu.SMEM), pl.BlockSpec(memory_space=pltpu.VMEM)],
        out_specs=pl.BlockSpec(memory_space=pl.ANY),
        scratch_shapes=[
            pltpu.VMEM((s4, NBLD, hours), jnp.bfloat16),
            pltpu.SemaphoreType.DMA((parts,)),
        ],
        compiler_params=pltpu.CompilerParams(vmem_limit_bytes=56 * 2**20),
        name="inverse",
    )(freq_index, pltpu.with_memory_space_constraint(wall, pltpu.VMEM))


def solution(mesh):
    nb, nz = mesh.shape["bore"], mesh.shape["freq"]

    def body(loads, pair_spectra, share, assignment, freq_index):
        owners = assignment.reshape(1, -1)
        wall = superpose(loads, pair_spectra, share, owners, freq_index, nb, nz)
        return inverse(freq_index, wall, loads.shape[0] // nz, loads.shape[2] * nz)

    return jax.shard_map(
        body,
        mesh=mesh,
        in_specs=(
            P("bore", None, "freq"),
            P("freq", None, "bore", None),
            P(None, "bore"),
            P(),
            P(),
        ),
        out_specs=P(("bore", "freq"), None, None),
        check_vma=False,
    )
```

```python
import functools
import math

import jax
import jax.numpy as jnp
from jax import lax
from jax.experimental import pallas as pl
from jax.experimental.pallas import tpu as pltpu
from jax.sharding import PartitionSpec as P

NBLD = 64
FLOC = 2
MESH = pl.DeviceIdType.MESH
NT = (((1,), (1,)), ((), ()))
TN = (((0,), (0,)), ((), ()))


def harmonic_column(freq_ref, freqs):
    row = lax.broadcasted_iota(jnp.int32, (freqs, 1), 0)
    column = jnp.zeros((freqs, 1), jnp.int32)
    for k in range(freqs):
        column = jnp.where(row == k, freq_ref[k], column)
    return column


def cos_sin(harmonics, first_hour, count, hours, stride=1):
    freqs = harmonics.shape[0]
    t = lax.broadcasted_iota(jnp.int32, (freqs, count), 1) * stride + first_hour
    phase = (harmonics * t) & (hours - 1)
    quarter = hours // 4
    turn = (phase + quarter // 2) // quarter
    x = (phase - turn * quarter).astype(jnp.float32) * (2.0 * math.pi / hours)
    y = x * x
    c = 1.0 + y * (-0.5 + y * (1 / 24 + y * (-1 / 720 + y * (1 / 40320 - y * (1 / 3628800)))))
    s = x * (1.0 + y * (-1 / 6 + y * (1 / 120 + y * (-1 / 5040 + y * (1 / 362880)))))
    odd = (turn & 1) == 1
    cos = jnp.where(odd, s, c)
    sin = jnp.where(odd, c, s)
    cos = jnp.where((turn == 1) | (turn == 2), -cos, cos)
    sin = jnp.where((turn == 2) | (turn == 3), -sin, sin)
    return cos, sin


def halves(x):
    upper = x.astype(jnp.bfloat16)
    return upper, (x - upper.astype(jnp.float32)).astype(jnp.bfloat16)


def superpose_kernel(
    nb, nz, hours, freq_ref, owner_ref, loads_hbm, pair_hbm, share_hbm, out_ref,
    loads_v, pair_v, share_v, sel_v, grid_v, cross_stage, cross_recv,
    bs_stage, bs_all, wall_stage, wall_recv,
    loads_sem, pair_sem, own_sem, sh_send, sh_recv, fw_send, fw_recv,
    cr_ssem, cr_rsem, bs_ssem, bs_rsem, wl_ssem, wl_rsem,
):
    b = lax.axis_index("bore")
    z = lax.axis_index("freq")
    sloc = loads_hbm.shape[0]
    tloc = loads_hbm.shape[2]
    freqs = freq_ref.shape[0]
    bores = owner_ref.shape[1]
    bloc = pair_hbm.shape[2]
    scenarios = share_hbm.shape[0]
    s4 = sloc // nz
    core = b % 2
    chip = b // 2
    chips = nb // 2
    sibling = b + 1 - 2 * core
    near_first = sorted(
        ((r, k) for r in range(nb) for k in range(nz) if r or k), key=lambda rk: min(rk[1], nz - rk[1])
    )

    own_share = pltpu.make_async_copy(share_hbm, share_v.at[b], own_sem)
    own_share.start()
    sp = sloc // 2
    hp = tloc // 2
    load_copies = [
        [
            pltpu.make_async_copy(
                loads_hbm.at[pl.ds(i * sp, sp), :, pl.ds(h * hp, hp)],
                loads_v.at[pl.ds(i * sp, sp), :, pl.ds(h * hp, hp)],
                loads_sem.at[i, h],
            )
            for h in range(2)
        ]
        for i in range(2)
    ]
    for copy in load_copies[0] + load_copies[1]:
        copy.start()
    barrier = pltpu.get_barrier_semaphore()
    for r, k in near_first:
        pl.semaphore_signal(barrier, inc=1, device_id=((b + r) % nb, (z + k) % nz), device_id_type=MESH)

    turns = (1 - core, core)
    pair_copies = [
        pltpu.make_async_copy(pair_hbm.at[turns[i], d], pair_v.at[turns[i], d], pair_sem.at[i, d])
        for i in range(FLOC)
        for d in range(2)
    ]

    cos, sin = cos_sin(harmonic_column(freq_ref, freqs), z * tloc, tloc, hours)
    table = jnp.concatenate([*halves(cos), *halves(sin)], 0)
    lanes = sp * NBLD
    keep = lax.broadcasted_iota(jnp.int32, (sp, lanes), 1) // NBLD == lax.broadcasted_iota(jnp.int32, (sp, lanes), 0)
    fold_from = lax.broadcasted_iota(jnp.int32, (lanes, 128), 0) % NBLD
    fold_to = lax.broadcasted_iota(jnp.int32, (lanes, 128), 1)
    folds = [(fold_from + c * NBLD == fold_to).astype(jnp.float32).astype(jnp.bfloat16) for c in range(2)]

    square = chips == 4
    over_x = chip + 1 - 2 * (chip % 2)
    over_y = (chip + 2) % chips
    first_hops = (over_x, over_y) if square else tuple((chip + r) % chips for r in range(1, chips))
    first_from = first_hops if square else tuple((chip + chips - r) % chips for r in range(1, chips))
    share_copies = [
        pltpu.make_async_remote_copy(
            src_ref=share_v.at[b], dst_ref=share_v.at[b], send_sem=sh_send.at[r], recv_sem=sh_recv.at[r],
            device_id=device, device_id_type=MESH,
        )
        for r, device in enumerate([(to * 2 + core, z) for to in first_hops] + [(sibling, z)])
    ]

    for q in range(nb):
        piece = pl.ds(q * bloc, bloc)
        label = lax.broadcasted_iota(jnp.int32, (2 * NBLD, bloc), 0) % NBLD
        sel_v[:, piece] = (label == owner_ref[:, piece]).astype(jnp.float32).astype(jnp.bfloat16)

    pl.semaphore_wait(barrier, nb * nz - 1)
    own_share.wait()
    for copy in share_copies:
        copy.start()

    folded = []
    for i in range(2):
        spec = jnp.zeros((4 * freqs, lanes), jnp.float32)
        for h in range(2):
            load_copies[i][h].wait()
            pair_copies[2 * i + h].start()
            chunk = loads_v[pl.ds(i * sp, sp), :, pl.ds(h * hp, hp)].reshape(lanes, hp)
            spec = spec + lax.dot_general(
                table[:, h * hp : (h + 1) * hp], chunk, NT, preferred_element_type=jnp.float32
            )
        total = jnp.zeros((freqs * sp, 128), jnp.float32)
        for c in range(2):
            upper, lower = spec[2 * c * freqs : (2 * c + 1) * freqs], spec[(2 * c + 1) * freqs : (2 * c + 2) * freqs]
            part = (upper + lower) * ((1.0 - 2.0 * c) / math.sqrt(hours))
            spread = jnp.concatenate(
                [jnp.where(keep, part[k : k + 1], 0.0).astype(jnp.bfloat16) for k in range(freqs)], 0
            )
            total = total + jnp.dot(spread, folds[c], preferred_element_type=jnp.float32)
        folded.append(total.reshape(freqs, sp, 128))
    bs_stage[...] = jnp.concatenate(folded, 1).astype(jnp.bfloat16)

    bs_copies = []
    for r, k in near_first[::-1]:
        to_b, to_z = (b + r) % nb, (z + k) % nz
        bs_copies.append(
            pltpu.make_async_remote_copy(
                src_ref=bs_stage.at[to_z * FLOC + to_b % 2], dst_ref=bs_all.at[z, b],
                send_sem=bs_ssem.at[r, k], recv_sem=bs_rsem.at[r, k],
                device_id=(to_b, to_z), device_id_type=MESH,
            )
        )
        bs_copies[-1].start()
    bs_all[z, b] = bs_stage[z * FLOC + core]

    fw_copies = []

    def forward(r, origin, rows, device):
        there = share_v.at[origin, rows]
        fw_copies.append(
            pltpu.make_async_remote_copy(
                src_ref=there, dst_ref=there, send_sem=fw_send.at[r], recv_sem=fw_recv.at[r],
                device_id=(device, z), device_id_type=MESH,
            )
        )
        fw_copies[-1].start()

    here = sel_v[0:NBLD, pl.ds(pl.multiple_of(b * bloc, 128), bloc)]
    width = 2048

    cross_copies = []

    def gather_away(d):
        pair_copies[d].wait()

        def step(i, carry):
            piece = pl.ds(pl.multiple_of(i * width, width), width)
            total = jnp.dot(here, pair_v[turns[0], d, :, piece], preferred_element_type=jnp.float32)
            cross_stage[d, :, piece] = total.astype(jnp.bfloat16)
            return carry

        lax.fori_loop(0, bores // width, step, 0)
        cross_copies.append(
            pltpu.make_async_remote_copy(
                src_ref=cross_stage.at[d], dst_ref=cross_recv.at[d], send_sem=cr_ssem.at[d], recv_sem=cr_rsem.at[d],
                device_id=(sibling, z), device_id_type=MESH,
            )
        )
        cross_copies[-1].start()

    def gather_here(d):
        pair_copies[2 + d].wait()
        cross_copies[d].wait_recv()

        def step(i, carry):
            piece = pl.ds(pl.multiple_of(i * width, width), width)
            total = jnp.dot(here, pair_v[turns[1], d, :, piece], preferred_element_type=jnp.float32)
            total = total + cross_recv[d, :, piece].astype(jnp.float32)
            grid_v[pl.ds(d * NBLD, NBLD), piece] = total.astype(jnp.bfloat16)
            return carry

        lax.fori_loop(0, bores // width, step, 0)

    gather_away(0)
    gather_away(1)

    every = slice(0, scenarios)
    for r, origin in enumerate(first_from):
        share_copies[r].wait_recv()
        if square:
            rows = pl.ds(r * (scenarios // 2), scenarios // 2)
            forward(chips + r, origin * 2 + core, rows, first_hops[1 - r] * 2 + core)
        forward(r, origin * 2 + core, every, sibling)


    gather_here(0)
    gather_here(1)

    share_copies[-1].wait_recv()
    for copy in (fw_copies[1], fw_copies[3]) if square else fw_copies:
        copy.wait_recv()
    for copy in bs_copies:
        copy.wait_recv()

    spec_all = bs_all[0].astype(jnp.float32)
    for k in range(1, nz):
        spec_all = spec_all + bs_all[k].astype(jnp.float32)
    spec_all = spec_all.reshape(scenarios, 128)
    half = lax.broadcasted_iota(jnp.int32, (scenarios, 128), 1) // NBLD
    spec_c = jnp.concatenate([jnp.where(half == c, spec_all, 0.0).astype(jnp.bfloat16) for c in range(2)], 0)

    def source_blocks(origins, walls):
        for q in origins:
            piece = pl.ds(pl.multiple_of(q * bloc, 128), bloc)
            weight = share_v[q].astype(jnp.float32)
            picked = jnp.dot(spec_c, sel_v[:, piece], preferred_element_type=jnp.float32)
            source = (picked.reshape(2, scenarios, bloc) * weight).astype(jnp.bfloat16).reshape(2 * scenarios, bloc)
            walls = walls + lax.dot_general(source, grid_v[:, piece], NT, preferred_element_type=jnp.float32)
        return walls

    walls = jnp.zeros((2 * scenarios, 128), jnp.float32)
    if square:
        diagonal = (over_x + 2) % chips * 2
        walls = source_blocks([b, sibling, over_x * 2, over_x * 2 + 1], walls)
        for r in range(2):
            fw_copies[2 * r].wait_recv()
        forward(2, diagonal + core, every, sibling)
        walls = source_blocks([over_y * 2, over_y * 2 + 1, diagonal + core], walls)
        fw_copies[4].wait_recv()
        walls = source_blocks([diagonal + 1 - core], walls)
    else:
        walls = source_blocks(range(nb), walls)
    sign = jnp.where(lax.broadcasted_iota(jnp.int32, (scenarios, 128), 1) < NBLD, -1.0, 1.0)
    joined = (walls[:scenarios] + sign * pltpu.roll(walls[scenarios:], NBLD, 1)) * (NBLD / bores)
    wall_stage[...] = joined.reshape(nb * nz, s4, 128)

    slot = z * FLOC + core
    def wall_copy(r, to_z, from_z):
        to_b = (b + r) % nb
        return pltpu.make_async_remote_copy(
            src_ref=wall_stage.at[to_b * nz + to_z], dst_ref=wall_recv.at[slot, chip],
            send_sem=wl_ssem.at[r, to_z], recv_sem=wl_rsem.at[r, from_z],
            device_id=(to_b, to_z), device_id_type=MESH,
        )

    plane_first = []
    for k in range(nz):
        plane_first += [(r, k) for r in range(1, nb)]
        if k < nz - 1:
            plane_first.append((0, k + (z <= k).astype(jnp.int32)))
    for r, k in plane_first:
        wall_copy(r, k, z).start()
    wall_recv[slot, chip] = wall_stage[b * nz + z]
    for copy in share_copies + bs_copies + fw_copies + cross_copies:
        copy.wait_send()
    for r, k in plane_first:
        wall_copy(r, k, k).wait()
    wall = wall_recv[:, 0]
    for q in range(1, chips):
        wall = wall + wall_recv[:, q]
    out_ref[...] = wall.reshape(freqs * s4, 128)


def superpose(loads, pair_spectra, share, owners, freq_index, nb, nz):
    sloc, _, tloc = loads.shape
    bloc, bores = pair_spectra.shape[2:]
    scenarios = share.shape[0]
    freqs = freq_index.shape[0]
    s4 = sloc // nz
    bf16, f32, dma = jnp.bfloat16, jnp.float32, pltpu.SemaphoreType.DMA
    anywhere = pl.BlockSpec(memory_space=pl.ANY)
    return pl.pallas_call(
        functools.partial(superpose_kernel, nb, nz, tloc * nz),
        out_shape=pltpu.VMEM((nz * FLOC * s4, 128), f32),
        in_specs=[
            pl.BlockSpec(memory_space=pltpu.SMEM),
            pl.BlockSpec(memory_space=pltpu.VMEM),
            anywhere,
            anywhere,
            anywhere,
        ],
        out_specs=pl.BlockSpec(memory_space=pltpu.VMEM),
        scratch_shapes=[
            pltpu.VMEM(loads.shape, bf16),
            pltpu.VMEM(pair_spectra.shape, bf16),
            pltpu.VMEM((nb, scenarios, bloc), bf16),
            pltpu.VMEM((2 * NBLD, bores), bf16),
            pltpu.VMEM((2 * NBLD, bores), bf16),
            pltpu.VMEM((2, NBLD, bores), bf16),
            pltpu.VMEM((2, NBLD, bores), bf16),
            pltpu.VMEM((freqs, sloc, 128), bf16),
            pltpu.VMEM((nz, nb, sloc, 128), bf16),
            pltpu.VMEM((nb * nz, s4, 128), f32),
            pltpu.VMEM((freqs, nb // 2, s4, 128), f32),
            dma((2, 2)),
            dma((FLOC, 2)),
            dma,
            dma((nb // 2,)),
            dma((nb // 2,)),
            dma((nb // 2 + 2,)),
            dma((nb // 2 + 2,)),
            dma((2,)),
            dma((2,)),
            dma((nb, nz)),
            dma((nb, nz)),
            dma((nb, nz)),
            dma((nb, nz)),
        ],
        compiler_params=pltpu.CompilerParams(
            collective_id=0, has_side_effects=True, vmem_limit_bytes=56 * 2**20
        ),
        name="superpose",
    )(freq_index, owners, loads, pair_spectra, share)


def inverse_kernel(hours, freq_ref, wall_v, out_hbm, out_v, out_sem):
    freqs = freq_ref.shape[0]
    s4 = out_hbm.shape[0]
    parts = out_sem.shape[0]
    count = hours // parts
    harmonics = harmonic_column(freq_ref, freqs)
    base_cos, base_sin = cos_sin(harmonics, 0, count, hours)
    turn_cos, turn_sin = cos_sin(harmonics, 0, 128, hours, count)
    low = lax.broadcasted_iota(jnp.int32, (freqs, 128), 1) < NBLD
    real, imag = [], []
    for s in range(0, s4, 2):
        one = wall_v[pl.ds(s, freqs, stride=s4), :]
        two = wall_v[pl.ds(s + 1, freqs, stride=s4), :]
        real.append(jnp.where(low, one, pltpu.roll(two, NBLD, 1)))
        imag.append(jnp.where(low, pltpu.roll(one, NBLD, 1), two))
    left = jnp.concatenate([jnp.concatenate(real, 1), -jnp.concatenate(imag, 1)], 0)
    upper, lower = halves(left * (1.0 / math.sqrt(freqs)))
    upper, lower = upper.astype(jnp.float32), lower.astype(jnp.float32)
    left = jnp.concatenate([upper, upper, lower], 0).T.astype(jnp.bfloat16)
    width = min(512, count)
    copies = []
    for i in range(parts):
        c, s = turn_cos[:, i : i + 1], turn_sin[:, i : i + 1]
        for j in range(0, count, width):
            piece = slice(j, j + width)
            cos = base_cos[:, piece] * c - base_sin[:, piece] * s
            sin = base_sin[:, piece] * c + base_cos[:, piece] * s
            upper, lower = halves(jnp.concatenate([cos, sin], 0))
            right = jnp.concatenate([upper, lower, upper], 0)
            total = jnp.dot(left, right, preferred_element_type=jnp.float32)
            out_v[:, :, pl.ds(i * count + j, width)] = total.astype(jnp.bfloat16).reshape(s4, NBLD, width)
        piece = pl.ds(i * count, count)
        copies.append(pltpu.make_async_copy(out_v.at[:, :, piece], out_hbm.at[:, :, piece], out_sem.at[i]))
        copies[-1].start()
    for copy in copies:
        copy.wait()


def inverse(freq_index, wall, s4, hours):
    parts = 8
    return pl.pallas_call(
        functools.partial(inverse_kernel, hours),
        out_shape=jax.ShapeDtypeStruct((s4, NBLD, hours), jnp.bfloat16),
        in_specs=[pl.BlockSpec(memory_space=pltpu.SMEM), pl.BlockSpec(memory_space=pltpu.VMEM)],
        out_specs=pl.BlockSpec(memory_space=pl.ANY),
        scratch_shapes=[
            pltpu.VMEM((s4, NBLD, hours), jnp.bfloat16),
            pltpu.SemaphoreType.DMA((parts,)),
        ],
        compiler_params=pltpu.CompilerParams(vmem_limit_bytes=56 * 2**20),
        name="inverse",
    )(freq_index, pltpu.with_memory_space_constraint(wall, pltpu.VMEM))


def solution(mesh):
    nb, nz = mesh.shape["bore"], mesh.shape["freq"]

    def body(loads, pair_spectra, share, assignment, freq_index):
        owners = assignment.reshape(1, -1)
        wall = superpose(loads, pair_spectra, share, owners, freq_index, nb, nz)
        return inverse(freq_index, wall, loads.shape[0] // nz, loads.shape[2] * nz)

    return jax.shard_map(
        body,
        mesh=mesh,
        in_specs=(
            P("bore", None, "freq"),
            P("freq", None, "bore", None),
            P(None, "bore"),
            P(),
            P(),
        ),
        out_specs=P(("bore", "freq"), None, None),
        check_vma=False,
    )
```

```python
import functools
import math

import jax
import jax.numpy as jnp
from jax import lax
from jax.experimental import pallas as pl
from jax.experimental.pallas import tpu as pltpu
from jax.sharding import PartitionSpec as P

NBLD = 64
FLOC = 2
MESH = pl.DeviceIdType.MESH
NT = (((1,), (1,)), ((), ()))
TN = (((0,), (0,)), ((), ()))


def harmonic_column(freq_ref, freqs):
    row = lax.broadcasted_iota(jnp.int32, (freqs, 1), 0)
    column = jnp.zeros((freqs, 1), jnp.int32)
    for k in range(freqs):
        column = jnp.where(row == k, freq_ref[k], column)
    return column


def cos_sin(harmonics, first_hour, count, hours, stride=1):
    freqs = harmonics.shape[0]
    t = lax.broadcasted_iota(jnp.int32, (freqs, count), 1) * stride + first_hour
    phase = (harmonics * t) & (hours - 1)
    quarter = hours // 4
    turn = (phase + quarter // 2) // quarter
    x = (phase - turn * quarter).astype(jnp.float32) * (2.0 * math.pi / hours)
    y = x * x
    c = 1.0 + y * (-0.5 + y * (1 / 24 + y * (-1 / 720 + y * (1 / 40320 - y * (1 / 3628800)))))
    s = x * (1.0 + y * (-1 / 6 + y * (1 / 120 + y * (-1 / 5040 + y * (1 / 362880)))))
    odd = (turn & 1) == 1
    cos = jnp.where(odd, s, c)
    sin = jnp.where(odd, c, s)
    cos = jnp.where((turn == 1) | (turn == 2), -cos, cos)
    sin = jnp.where((turn == 2) | (turn == 3), -sin, sin)
    return cos, sin


def halves(x):
    upper = x.astype(jnp.bfloat16)
    return upper, (x - upper.astype(jnp.float32)).astype(jnp.bfloat16)


def superpose_kernel(
    nb, nz, hours, freq_ref, owner_ref, loads_hbm, pair_hbm, share_hbm, out_ref,
    loads_v, pair_v, share_v, sel_v, grid_v, cross_stage, cross_recv,
    bs_stage, bs_all, wall_stage, wall_recv,
    loads_sem, pair_sem, own_sem, sh_send, sh_recv, fw_send, fw_recv,
    cr_ssem, cr_rsem, bs_ssem, bs_rsem, wl_ssem, wl_rsem,
):
    b = lax.axis_index("bore")
    z = lax.axis_index("freq")
    sloc = loads_hbm.shape[0]
    tloc = loads_hbm.shape[2]
    freqs = freq_ref.shape[0]
    bores = owner_ref.shape[1]
    bloc = pair_hbm.shape[2]
    scenarios = share_hbm.shape[0]
    s4 = sloc // nz
    core = b % 2
    chip = b // 2
    chips = nb // 2
    sibling = b + 1 - 2 * core
    near_first = sorted(
        ((r, k) for r in range(nb) for k in range(nz) if r or k), key=lambda rk: min(rk[1], nz - rk[1])
    )

    own_share = pltpu.make_async_copy(share_hbm, share_v.at[b], own_sem)
    own_share.start()
    sp = sloc // 2
    hp = tloc // 2
    load_copies = [
        [
            pltpu.make_async_copy(
                loads_hbm.at[pl.ds(i * sp, sp), :, pl.ds(h * hp, hp)],
                loads_v.at[pl.ds(i * sp, sp), :, pl.ds(h * hp, hp)],
                loads_sem.at[i, h],
            )
            for h in range(2)
        ]
        for i in range(2)
    ]
    for copy in load_copies[0] + load_copies[1]:
        copy.start()
    barrier = pltpu.get_barrier_semaphore()
    for r, k in near_first:
        pl.semaphore_signal(barrier, inc=1, device_id=((b + r) % nb, (z + k) % nz), device_id_type=MESH)

    turns = (1 - core, core)
    pair_copies = [
        pltpu.make_async_copy(pair_hbm.at[turns[i], d], pair_v.at[turns[i], d], pair_sem.at[i, d])
        for i in range(FLOC)
        for d in range(2)
    ]

    cos, sin = cos_sin(harmonic_column(freq_ref, freqs), z * tloc, tloc, hours)
    table = jnp.concatenate([*halves(cos), *halves(sin)], 0)
    lanes = sp * NBLD
    square = chips == 4
    over_x = chip + 1 - 2 * (chip % 2)
    over_y = (chip + 2) % chips
    first_hops = (over_x, over_y) if square else tuple((chip + r) % chips for r in range(1, chips))
    first_from = first_hops if square else tuple((chip + chips - r) % chips for r in range(1, chips))
    every = slice(0, scenarios)
    halves_of = [pl.ds(r * (scenarios // 2), scenarios // 2) for r in range(2)]
    if square:
        sends = [(halves_of[r], over) for r, over in enumerate(first_hops)]
        sends += [(halves_of[1 - r], over) for r, over in enumerate(first_hops)]
    else:
        sends = [(every, over) for over in first_hops]
    share_copies = [
        pltpu.make_async_remote_copy(
            src_ref=share_v.at[b, rows], dst_ref=share_v.at[b, rows], send_sem=sh_send.at[r], recv_sem=sh_recv.at[r],
            device_id=device, device_id_type=MESH,
        )
        for r, (rows, device) in enumerate(
            [(rows, (over * 2 + core, z)) for rows, over in sends] + [(every, (sibling, z))]
        )
    ]
    for q in range(nb):
        piece = pl.ds(q * bloc, bloc)
        label = lax.broadcasted_iota(jnp.int32, (2 * NBLD, bloc), 0) % NBLD
        sel_v[:, piece] = (label == owner_ref[:, piece]).astype(jnp.float32).astype(jnp.bfloat16)

    pl.semaphore_wait(barrier, nb * nz - 1)
    own_share.wait()
    for copy in share_copies:
        copy.start()

    folded = []
    for i in range(2):
        spec = jnp.zeros((4 * freqs, lanes), jnp.float32)
        for h in range(2):
            load_copies[i][h].wait()
            pair_copies[2 * i + h].start()
            chunk = loads_v[pl.ds(i * sp, sp), :, pl.ds(h * hp, hp)].reshape(lanes, hp)
            spec = spec + lax.dot_general(
                table[:, h * hp : (h + 1) * hp], chunk, NT, preferred_element_type=jnp.float32
            )
        real = (spec[:freqs] + spec[freqs : 2 * freqs]) * (1.0 / math.sqrt(hours))
        imag = (spec[2 * freqs : 3 * freqs] + spec[3 * freqs :]) * (-1.0 / math.sqrt(hours))
        rows = [
            jnp.concatenate([part[:, r * NBLD : (r + 1) * NBLD] for part in (real, imag)], 1)[None]
            for r in range(sp)
        ]
        folded.append(jnp.swapaxes(jnp.concatenate(rows, 0), 0, 1))
    bs_stage[...] = jnp.concatenate(folded, 1).astype(jnp.bfloat16)

    bs_copies = []
    for r, k in near_first[::-1]:
        to_b, to_z = (b + r) % nb, (z + k) % nz
        bs_copies.append(
            pltpu.make_async_remote_copy(
                src_ref=bs_stage.at[to_z * FLOC + to_b % 2], dst_ref=bs_all.at[z, b],
                send_sem=bs_ssem.at[r, k], recv_sem=bs_rsem.at[r, k],
                device_id=(to_b, to_z), device_id_type=MESH,
            )
        )
        bs_copies[-1].start()
    bs_all[z, b] = bs_stage[z * FLOC + core]

    here = sel_v[0:NBLD, pl.ds(pl.multiple_of(b * bloc, 128), bloc)]
    width = 2048

    cross_copies = []

    def gather_away(d):
        pair_copies[d].wait()

        def step(i, carry):
            piece = pl.ds(pl.multiple_of(i * width, width), width)
            total = jnp.dot(here, pair_v[turns[0], d, :, piece], preferred_element_type=jnp.float32)
            cross_stage[d, :, piece] = total.astype(jnp.bfloat16)
            return carry

        lax.fori_loop(0, bores // width, step, 0)
        cross_copies.append(
            pltpu.make_async_remote_copy(
                src_ref=cross_stage.at[d], dst_ref=cross_recv.at[d], send_sem=cr_ssem.at[d], recv_sem=cr_rsem.at[d],
                device_id=(sibling, z), device_id_type=MESH,
            )
        )
        cross_copies[-1].start()

    def gather_here(d):
        pair_copies[2 + d].wait()
        cross_copies[d].wait_recv()

        def step(i, carry):
            piece = pl.ds(pl.multiple_of(i * width, width), width)
            total = jnp.dot(here, pair_v[turns[1], d, :, piece], preferred_element_type=jnp.float32)
            total = total + cross_recv[d, :, piece].astype(jnp.float32)
            grid_v[pl.ds(d * NBLD, NBLD), piece] = total.astype(jnp.bfloat16)
            return carry

        lax.fori_loop(0, bores // width, step, 0)

    gather_away(0)

    fw_copies = []

    def forward(r, origin, rows, device):
        there = share_v.at[origin, rows]
        fw_copies.append(
            pltpu.make_async_remote_copy(
                src_ref=there, dst_ref=there, send_sem=fw_send.at[r], recv_sem=fw_recv.at[r],
                device_id=(device, z), device_id_type=MESH,
            )
        )
        fw_copies[-1].start()

    if square:
        for r, origin in enumerate(first_from):
            share_copies[r].wait_recv()
            forward(chips + r, origin * 2 + core, halves_of[r], first_hops[1 - r] * 2 + core)

    gather_away(1)

    gather_here(0)

    for r, origin in enumerate(first_from):
        share_copies[2 + r if square else r].wait_recv()
        forward(r, origin * 2 + core, every, sibling)

    gather_here(1)

    if square:
        diagonal = (over_x + 2) % chips * 2
        for r in range(2):
            fw_copies[r].wait_recv()
        forward(2, diagonal + core, every, sibling)
    share_copies[-1].wait_recv()
    for copy in fw_copies[2:4] if square else fw_copies:
        copy.wait_recv()
    for copy in bs_copies:
        copy.wait_recv()

    spec_all = bs_all[0].astype(jnp.float32)
    for k in range(1, nz):
        spec_all = spec_all + bs_all[k].astype(jnp.float32)
    spec_all = spec_all.reshape(scenarios, 128)
    half = lax.broadcasted_iota(jnp.int32, (scenarios, 128), 1) // NBLD
    spec_c = jnp.concatenate([jnp.where(half == c, spec_all, 0.0).astype(jnp.bfloat16) for c in range(2)], 0)

    def source_blocks(origins, walls):
        for q in origins:
            piece = pl.ds(pl.multiple_of(q * bloc, 128), bloc)
            weight = share_v[q].astype(jnp.float32)
            picked = jnp.dot(spec_c, sel_v[:, piece], preferred_element_type=jnp.float32)
            source = (picked.reshape(2, scenarios, bloc) * weight).astype(jnp.bfloat16).reshape(2 * scenarios, bloc)
            walls = walls + lax.dot_general(source, grid_v[:, piece], NT, preferred_element_type=jnp.float32)
        return walls

    walls = jnp.zeros((2 * scenarios, 128), jnp.float32)
    if square:
        walls = source_blocks([b, sibling, over_x * 2, over_x * 2 + 1, over_y * 2, over_y * 2 + 1, diagonal + core], walls)
        fw_copies[4].wait_recv()
        walls = source_blocks([diagonal + 1 - core], walls)
    else:
        walls = source_blocks(range(nb), walls)
    sign = jnp.where(lax.broadcasted_iota(jnp.int32, (scenarios, 128), 1) < NBLD, -1.0, 1.0)
    joined = (walls[:scenarios] + sign * pltpu.roll(walls[scenarios:], NBLD, 1)) * (NBLD / bores)
    wall_stage[...] = joined.reshape(nb * nz, s4, 128)

    slot = z * FLOC + core
    def wall_copy(r, to_z, from_z):
        to_b = (b + r) % nb
        return pltpu.make_async_remote_copy(
            src_ref=wall_stage.at[to_b * nz + to_z], dst_ref=wall_recv.at[slot, chip],
            send_sem=wl_ssem.at[r, to_z], recv_sem=wl_rsem.at[r, from_z],
            device_id=(to_b, to_z), device_id_type=MESH,
        )

    plane_first = []
    for k in range(nz):
        plane_first += [(r, k) for r in range(1, nb)]
        if k < nz - 1:
            plane_first.append((0, k + (z <= k).astype(jnp.int32)))
    for r, k in plane_first:
        wall_copy(r, k, z).start()
    wall_recv[slot, chip] = wall_stage[b * nz + z]
    for copy in share_copies + bs_copies + fw_copies + cross_copies:
        copy.wait_send()
    for r, k in plane_first:
        wall_copy(r, k, k).wait()
    wall = wall_recv[:, 0]
    for q in range(1, chips):
        wall = wall + wall_recv[:, q]
    out_ref[...] = wall.reshape(freqs * s4, 128)


def superpose(loads, pair_spectra, share, owners, freq_index, nb, nz):
    sloc, _, tloc = loads.shape
    bloc, bores = pair_spectra.shape[2:]
    scenarios = share.shape[0]
    freqs = freq_index.shape[0]
    s4 = sloc // nz
    bf16, f32, dma = jnp.bfloat16, jnp.float32, pltpu.SemaphoreType.DMA
    anywhere = pl.BlockSpec(memory_space=pl.ANY)
    return pl.pallas_call(
        functools.partial(superpose_kernel, nb, nz, tloc * nz),
        out_shape=pltpu.VMEM((nz * FLOC * s4, 128), f32),
        in_specs=[
            pl.BlockSpec(memory_space=pltpu.SMEM),
            pl.BlockSpec(memory_space=pltpu.VMEM),
            anywhere,
            anywhere,
            anywhere,
        ],
        out_specs=pl.BlockSpec(memory_space=pltpu.VMEM),
        scratch_shapes=[
            pltpu.VMEM(loads.shape, bf16),
            pltpu.VMEM(pair_spectra.shape, bf16),
            pltpu.VMEM((nb, scenarios, bloc), bf16),
            pltpu.VMEM((2 * NBLD, bores), bf16),
            pltpu.VMEM((2 * NBLD, bores), bf16),
            pltpu.VMEM((2, NBLD, bores), bf16),
            pltpu.VMEM((2, NBLD, bores), bf16),
            pltpu.VMEM((freqs, sloc, 128), bf16),
            pltpu.VMEM((nz, nb, sloc, 128), bf16),
            pltpu.VMEM((nb * nz, s4, 128), f32),
            pltpu.VMEM((freqs, nb // 2, s4, 128), f32),
            dma((2, 2)),
            dma((FLOC, 2)),
            dma,
            dma((nb // 2 + 1,)),
            dma((nb // 2 + 1,)),
            dma((nb // 2 + 2,)),
            dma((nb // 2 + 2,)),
            dma((2,)),
            dma((2,)),
            dma((nb, nz)),
            dma((nb, nz)),
            dma((nb, nz)),
            dma((nb, nz)),
        ],
        compiler_params=pltpu.CompilerParams(
            collective_id=0, has_side_effects=True, vmem_limit_bytes=56 * 2**20
        ),
        name="superpose",
    )(freq_index, owners, loads, pair_spectra, share)


def inverse_kernel(hours, freq_ref, wall_v, out_hbm, out_v, out_sem):
    freqs = freq_ref.shape[0]
    s4 = out_hbm.shape[0]
    parts = out_sem.shape[0]
    count = hours // parts
    harmonics = harmonic_column(freq_ref, freqs)
    base_cos, base_sin = cos_sin(harmonics, 0, count, hours)
    turn_cos, turn_sin = cos_sin(harmonics, 0, 128, hours, count)
    low = lax.broadcasted_iota(jnp.int32, (freqs, 128), 1) < NBLD
    real, imag = [], []
    for s in range(0, s4, 2):
        one = wall_v[pl.ds(s, freqs, stride=s4), :]
        two = wall_v[pl.ds(s + 1, freqs, stride=s4), :]
        real.append(jnp.where(low, one, pltpu.roll(two, NBLD, 1)))
        imag.append(jnp.where(low, pltpu.roll(one, NBLD, 1), two))
    left = jnp.concatenate([jnp.concatenate(real, 1), -jnp.concatenate(imag, 1)], 0)
    upper, lower = halves(left * (1.0 / math.sqrt(freqs)))
    upper, lower = upper.astype(jnp.float32), lower.astype(jnp.float32)
    left = jnp.concatenate([upper, upper, lower], 0).T.astype(jnp.bfloat16)
    width = min(512, count)
    copies = []
    for i in range(parts):
        c, s = turn_cos[:, i : i + 1], turn_sin[:, i : i + 1]
        for j in range(0, count, width):
            piece = slice(j, j + width)
            cos = base_cos[:, piece] * c - base_sin[:, piece] * s
            sin = base_sin[:, piece] * c + base_cos[:, piece] * s
            upper, lower = halves(jnp.concatenate([cos, sin], 0))
            right = jnp.concatenate([upper, lower, upper], 0)
            total = jnp.dot(left, right, preferred_element_type=jnp.float32)
            out_v[:, :, pl.ds(i * count + j, width)] = total.astype(jnp.bfloat16).reshape(s4, NBLD, width)
        piece = pl.ds(i * count, count)
        copies.append(pltpu.make_async_copy(out_v.at[:, :, piece], out_hbm.at[:, :, piece], out_sem.at[i]))
        copies[-1].start()
    for copy in copies:
        copy.wait()


def inverse(freq_index, wall, s4, hours):
    parts = 8
    return pl.pallas_call(
        functools.partial(inverse_kernel, hours),
        out_shape=jax.ShapeDtypeStruct((s4, NBLD, hours), jnp.bfloat16),
        in_specs=[pl.BlockSpec(memory_space=pltpu.SMEM), pl.BlockSpec(memory_space=pltpu.VMEM)],
        out_specs=pl.BlockSpec(memory_space=pl.ANY),
        scratch_shapes=[
            pltpu.VMEM((s4, NBLD, hours), jnp.bfloat16),
            pltpu.SemaphoreType.DMA((parts,)),
        ],
        compiler_params=pltpu.CompilerParams(vmem_limit_bytes=56 * 2**20),
        name="inverse",
    )(freq_index, pltpu.with_memory_space_constraint(wall, pltpu.VMEM))


def solution(mesh):
    nb, nz = mesh.shape["bore"], mesh.shape["freq"]

    def body(loads, pair_spectra, share, assignment, freq_index):
        owners = assignment.reshape(1, -1)
        wall = superpose(loads, pair_spectra, share, owners, freq_index, nb, nz)
        return inverse(freq_index, wall, loads.shape[0] // nz, loads.shape[2] * nz)

    return jax.shard_map(
        body,
        mesh=mesh,
        in_specs=(
            P("bore", None, "freq"),
            P("freq", None, "bore", None),
            P(None, "bore"),
            P(),
            P(),
        ),
        out_specs=P(("bore", "freq"), None, None),
        check_vma=False,
    )
```

```python
import functools
import math

import jax
import jax.numpy as jnp
from jax import lax
from jax.experimental import pallas as pl
from jax.experimental.pallas import tpu as pltpu
from jax.sharding import PartitionSpec as P

NBLD = 64
FLOC = 2
MESH = pl.DeviceIdType.MESH
NT = (((1,), (1,)), ((), ()))
TN = (((0,), (0,)), ((), ()))


def harmonic_column(freq_ref, freqs):
    row = lax.broadcasted_iota(jnp.int32, (freqs, 1), 0)
    column = jnp.zeros((freqs, 1), jnp.int32)
    for k in range(freqs):
        column = jnp.where(row == k, freq_ref[k], column)
    return column


def cos_sin(harmonics, first_hour, count, hours, stride=1):
    freqs = harmonics.shape[0]
    t = lax.broadcasted_iota(jnp.int32, (freqs, count), 1) * stride + first_hour
    phase = (harmonics * t) & (hours - 1)
    quarter = hours // 4
    turn = (phase + quarter // 2) // quarter
    x = (phase - turn * quarter).astype(jnp.float32) * (2.0 * math.pi / hours)
    y = x * x
    c = 1.0 + y * (-0.5 + y * (1 / 24 + y * (-1 / 720 + y * (1 / 40320 - y * (1 / 3628800)))))
    s = x * (1.0 + y * (-1 / 6 + y * (1 / 120 + y * (-1 / 5040 + y * (1 / 362880)))))
    odd = (turn & 1) == 1
    cos = jnp.where(odd, s, c)
    sin = jnp.where(odd, c, s)
    cos = jnp.where((turn == 1) | (turn == 2), -cos, cos)
    sin = jnp.where((turn == 2) | (turn == 3), -sin, sin)
    return cos, sin


def halves(x):
    upper = x.astype(jnp.bfloat16)
    return upper, (x - upper.astype(jnp.float32)).astype(jnp.bfloat16)


def superpose_kernel(
    nb, nz, hours, freq_ref, owner_ref, loads_hbm, pair_hbm, share_hbm, out_ref,
    loads_v, pair_v, share_v, sel_v, grid_v, cross_stage, cross_recv,
    bs_stage, bs_all, wall_stage, wall_recv,
    loads_sem, pair_sem, own_sem, sh_send, sh_recv, fw_send, fw_recv,
    cr_ssem, cr_rsem, bs_ssem, bs_rsem, wl_ssem, wl_rsem,
):
    b = lax.axis_index("bore")
    z = lax.axis_index("freq")
    sloc = loads_hbm.shape[0]
    tloc = loads_hbm.shape[2]
    freqs = freq_ref.shape[0]
    bores = owner_ref.shape[1]
    bloc = pair_hbm.shape[2]
    scenarios = share_hbm.shape[0]
    s4 = sloc // nz
    core = b % 2
    chip = b // 2
    chips = nb // 2
    sibling = b + 1 - 2 * core
    near_first = sorted(
        ((r, k) for r in range(nb) for k in range(nz) if r or k), key=lambda rk: min(rk[1], nz - rk[1])
    )

    own_share = pltpu.make_async_copy(share_hbm, share_v.at[b], own_sem)
    own_share.start()
    sp = sloc // 2
    hp = tloc // 2
    load_copies = [
        [
            pltpu.make_async_copy(
                loads_hbm.at[pl.ds(i * sp, sp), :, pl.ds(h * hp, hp)],
                loads_v.at[pl.ds(i * sp, sp), :, pl.ds(h * hp, hp)],
                loads_sem.at[i, h],
            )
            for h in range(2)
        ]
        for i in range(2)
    ]
    for copy in load_copies[0] + load_copies[1]:
        copy.start()
    barrier = pltpu.get_barrier_semaphore()
    for r, k in near_first:
        pl.semaphore_signal(barrier, inc=1, device_id=((b + r) % nb, (z + k) % nz), device_id_type=MESH)

    turns = (1 - core, core)
    pair_copies = [
        pltpu.make_async_copy(pair_hbm.at[turns[i], d], pair_v.at[turns[i], d], pair_sem.at[i, d])
        for i in range(FLOC)
        for d in range(2)
    ]

    cos, sin = cos_sin(harmonic_column(freq_ref, freqs), z * tloc, tloc, hours)
    table = jnp.concatenate([*halves(cos), *halves(sin)], 0)
    lanes = sp * NBLD
    square = chips == 4
    over_x = chip + 1 - 2 * (chip % 2)
    over_y = (chip + 2) % chips
    first_hops = (over_x, over_y) if square else tuple((chip + r) % chips for r in range(1, chips))
    first_from = first_hops if square else tuple((chip + chips - r) % chips for r in range(1, chips))
    every = slice(0, scenarios)
    halves_of = [pl.ds(r * (scenarios // 2), scenarios // 2) for r in range(2)]
    if square:
        sends = [(halves_of[r], over) for r, over in enumerate(first_hops)]
        sends += [(halves_of[1 - r], over) for r, over in enumerate(first_hops)]
    else:
        sends = [(every, over) for over in first_hops]
    share_copies = [
        pltpu.make_async_remote_copy(
            src_ref=share_v.at[b, rows], dst_ref=share_v.at[b, rows], send_sem=sh_send.at[r], recv_sem=sh_recv.at[r],
            device_id=device, device_id_type=MESH,
        )
        for r, (rows, device) in enumerate(
            [(rows, (over * 2 + core, z)) for rows, over in sends] + [(every, (sibling, z))]
        )
    ]
    for q in range(nb):
        piece = pl.ds(q * bloc, bloc)
        label = lax.broadcasted_iota(jnp.int32, (2 * NBLD, bloc), 0) % NBLD
        sel_v[:, piece] = (label == owner_ref[:, piece]).astype(jnp.float32).astype(jnp.bfloat16)

    pl.semaphore_wait(barrier, nb * nz - 1)
    own_share.wait()
    for copy in share_copies:
        copy.start()

    folded = []
    for i in range(2):
        spec = jnp.zeros((4 * freqs, lanes), jnp.float32)
        for h in range(2):
            load_copies[i][h].wait()
            pair_copies[2 * i + h].start()
            chunk = loads_v[pl.ds(i * sp, sp), :, pl.ds(h * hp, hp)].reshape(lanes, hp)
            spec = spec + lax.dot_general(
                table[:, h * hp : (h + 1) * hp], chunk, NT, preferred_element_type=jnp.float32
            )
        real = (spec[:freqs] + spec[freqs : 2 * freqs]) * (1.0 / math.sqrt(hours))
        imag = (spec[2 * freqs : 3 * freqs] + spec[3 * freqs :]) * (-1.0 / math.sqrt(hours))
        rows = [
            jnp.concatenate([part[:, r * NBLD : (r + 1) * NBLD] for part in (real, imag)], 1)[None]
            for r in range(sp)
        ]
        folded.append(jnp.swapaxes(jnp.concatenate(rows, 0), 0, 1))
    bs_stage[...] = jnp.concatenate(folded, 1).astype(jnp.bfloat16)

    bs_copies = []
    for r, k in near_first[::-1]:
        to_b, to_z = (b + r) % nb, (z + k) % nz
        bs_copies.append(
            pltpu.make_async_remote_copy(
                src_ref=bs_stage.at[to_z * FLOC + to_b % 2], dst_ref=bs_all.at[z, b],
                send_sem=bs_ssem.at[r, k], recv_sem=bs_rsem.at[r, k],
                device_id=(to_b, to_z), device_id_type=MESH,
            )
        )
        bs_copies[-1].start()
    bs_all[z, b] = bs_stage[z * FLOC + core]

    here = sel_v[0:NBLD, pl.ds(pl.multiple_of(b * bloc, 128), bloc)]
    width = 2048

    cross_copies = []

    def gather_away(d):
        pair_copies[d].wait()

        def step(i, carry):
            piece = pl.ds(pl.multiple_of(i * width, width), width)
            total = jnp.dot(here, pair_v[turns[0], d, :, piece], preferred_element_type=jnp.float32)
            cross_stage[d, :, piece] = total.astype(jnp.bfloat16)
            return carry

        lax.fori_loop(0, bores // width, step, 0)
        cross_copies.append(
            pltpu.make_async_remote_copy(
                src_ref=cross_stage.at[d], dst_ref=cross_recv.at[d], send_sem=cr_ssem.at[d], recv_sem=cr_rsem.at[d],
                device_id=(sibling, z), device_id_type=MESH,
            )
        )
        cross_copies[-1].start()

    def gather_here(d):
        pair_copies[2 + d].wait()
        cross_copies[d].wait_recv()

        def step(i, carry):
            piece = pl.ds(pl.multiple_of(i * width, width), width)
            total = jnp.dot(here, pair_v[turns[1], d, :, piece], preferred_element_type=jnp.float32)
            total = total + cross_recv[d, :, piece].astype(jnp.float32)
            grid_v[pl.ds(d * NBLD, NBLD), piece] = total.astype(jnp.bfloat16)
            return carry

        lax.fori_loop(0, bores // width, step, 0)

    gather_away(0)

    fw_copies = []

    def forward(r, origin, rows, device):
        there = share_v.at[origin, rows]
        fw_copies.append(
            pltpu.make_async_remote_copy(
                src_ref=there, dst_ref=there, send_sem=fw_send.at[r], recv_sem=fw_recv.at[r],
                device_id=(device, z), device_id_type=MESH,
            )
        )
        fw_copies[-1].start()

    if square:
        for r, origin in enumerate(first_from):
            share_copies[r].wait_recv()
            forward(chips + r, origin * 2 + core, halves_of[r], first_hops[1 - r] * 2 + core)

    gather_away(1)

    gather_here(0)

    for r, origin in enumerate(first_from):
        share_copies[2 + r if square else r].wait_recv()
        forward(r, origin * 2 + core, every, sibling)

    gather_here(1)

    if square:
        diagonal = (over_x + 2) % chips * 2
        for r in range(2):
            fw_copies[r].wait_recv()
        forward(2, diagonal + core, every, sibling)
    share_copies[-1].wait_recv()
    for copy in fw_copies[2:4] if square else fw_copies:
        copy.wait_recv()
    for copy in bs_copies:
        copy.wait_recv()

    spec_all = bs_all[0].astype(jnp.float32)
    for k in range(1, nz):
        spec_all = spec_all + bs_all[k].astype(jnp.float32)
    spec_all = spec_all.reshape(scenarios, 128)
    half = lax.broadcasted_iota(jnp.int32, (scenarios, 128), 1) // NBLD
    sign = jnp.where(lax.broadcasted_iota(jnp.int32, (scenarios // 2, 128), 1) < NBLD, -1.0, 1.0)
    slot = z * FLOC + core
    me = b * nz + z
    others = [j + (me <= j).astype(jnp.int32) for j in range(nb * nz - 1)]

    def wall_copy(to, source):
        return pltpu.make_async_remote_copy(
            src_ref=wall_stage.at[to], dst_ref=wall_recv.at[slot, chip],
            send_sem=wl_ssem.at[to], recv_sem=wl_rsem.at[source],
            device_id=(to // nz, to % nz), device_id_type=MESH,
        )

    def source_blocks(part, origins, walls):
        rows = slice(part * (scenarios // 2), (part + 1) * (scenarios // 2))
        spec_c = jnp.concatenate(
            [jnp.where(half[rows] == c, spec_all[rows], 0.0).astype(jnp.bfloat16) for c in range(2)], 0
        )
        for q in origins:
            piece = pl.ds(pl.multiple_of(q * bloc, 128), bloc)
            weight = share_v[q, rows].astype(jnp.float32)
            picked = jnp.dot(spec_c, sel_v[:, piece], preferred_element_type=jnp.float32)
            source = (picked.reshape(2, scenarios // 2, bloc) * weight).astype(jnp.bfloat16).reshape(scenarios, bloc)
            walls = walls + lax.dot_general(source, grid_v[:, piece], NT, preferred_element_type=jnp.float32)
        return walls

    mid = nb * nz // 2
    for part in range(2):
        walls = jnp.zeros((scenarios, 128), jnp.float32)
        if square and part == 0:
            near = [q * 2 + c for q in (chip, over_x, over_y) for c in range(2)]
            walls = source_blocks(part, [*near, diagonal + core], walls)
            fw_copies[4].wait_recv()
            walls = source_blocks(part, [diagonal + 1 - core], walls)
        else:
            walls = source_blocks(part, range(nb), walls)
        joined = walls[: scenarios // 2] + sign * pltpu.roll(walls[scenarios // 2 :], NBLD, 1)
        wall_stage[pl.ds(part * mid, mid)] = (joined * (NBLD / bores)).reshape(mid, s4, 128)
        for to in others[mid - 1 :] if part else others[: mid - 1]:
            wall_copy(to, me).start()
    wall_recv[slot, chip] = wall_stage[b * nz + z]
    for copy in share_copies + bs_copies + fw_copies + cross_copies:
        copy.wait_send()
    for other in others:
        wall_copy(other, other).wait()
    wall = wall_recv[:, 0]
    for q in range(1, chips):
        wall = wall + wall_recv[:, q]
    out_ref[...] = wall.reshape(freqs * s4, 128)


def superpose(loads, pair_spectra, share, owners, freq_index, nb, nz):
    sloc, _, tloc = loads.shape
    bloc, bores = pair_spectra.shape[2:]
    scenarios = share.shape[0]
    freqs = freq_index.shape[0]
    s4 = sloc // nz
    bf16, f32, dma = jnp.bfloat16, jnp.float32, pltpu.SemaphoreType.DMA
    anywhere = pl.BlockSpec(memory_space=pl.ANY)
    return pl.pallas_call(
        functools.partial(superpose_kernel, nb, nz, tloc * nz),
        out_shape=pltpu.VMEM((nz * FLOC * s4, 128), f32),
        in_specs=[
            pl.BlockSpec(memory_space=pltpu.SMEM),
            pl.BlockSpec(memory_space=pltpu.VMEM),
            anywhere,
            anywhere,
            anywhere,
        ],
        out_specs=pl.BlockSpec(memory_space=pltpu.VMEM),
        scratch_shapes=[
            pltpu.VMEM(loads.shape, bf16),
            pltpu.VMEM(pair_spectra.shape, bf16),
            pltpu.VMEM((nb, scenarios, bloc), bf16),
            pltpu.VMEM((2 * NBLD, bores), bf16),
            pltpu.VMEM((2 * NBLD, bores), bf16),
            pltpu.VMEM((2, NBLD, bores), bf16),
            pltpu.VMEM((2, NBLD, bores), bf16),
            pltpu.VMEM((freqs, sloc, 128), bf16),
            pltpu.VMEM((nz, nb, sloc, 128), bf16),
            pltpu.VMEM((nb * nz, s4, 128), f32),
            pltpu.VMEM((freqs, nb // 2, s4, 128), f32),
            dma((2, 2)),
            dma((FLOC, 2)),
            dma,
            dma((nb // 2 + 1,)),
            dma((nb // 2 + 1,)),
            dma((nb // 2 + 2,)),
            dma((nb // 2 + 2,)),
            dma((2,)),
            dma((2,)),
            dma((nb, nz)),
            dma((nb, nz)),
            dma((nb * nz,)),
            dma((nb * nz,)),
        ],
        compiler_params=pltpu.CompilerParams(
            collective_id=0, has_side_effects=True, vmem_limit_bytes=56 * 2**20
        ),
        name="superpose",
    )(freq_index, owners, loads, pair_spectra, share)


def inverse_kernel(hours, freq_ref, wall_v, out_hbm, out_v, out_sem):
    freqs = freq_ref.shape[0]
    s4 = out_hbm.shape[0]
    parts = out_sem.shape[0]
    count = hours // parts
    harmonics = harmonic_column(freq_ref, freqs)
    base_cos, base_sin = cos_sin(harmonics, 0, count, hours)
    turn_cos, turn_sin = cos_sin(harmonics, 0, 128, hours, count)
    low = lax.broadcasted_iota(jnp.int32, (freqs, 128), 1) < NBLD
    real, imag = [], []
    for s in range(0, s4, 2):
        one = wall_v[pl.ds(s, freqs, stride=s4), :]
        two = wall_v[pl.ds(s + 1, freqs, stride=s4), :]
        real.append(jnp.where(low, one, pltpu.roll(two, NBLD, 1)))
        imag.append(jnp.where(low, pltpu.roll(one, NBLD, 1), two))
    left = jnp.concatenate([jnp.concatenate(real, 1), -jnp.concatenate(imag, 1)], 0)
    upper, lower = halves(left * (1.0 / math.sqrt(freqs)))
    upper, lower = upper.astype(jnp.float32), lower.astype(jnp.float32)
    left = jnp.concatenate([upper, upper, lower], 0).T.astype(jnp.bfloat16)
    width = min(512, count)
    copies = []
    for i in range(parts):
        c, s = turn_cos[:, i : i + 1], turn_sin[:, i : i + 1]
        for j in range(0, count, width):
            piece = slice(j, j + width)
            cos = base_cos[:, piece] * c - base_sin[:, piece] * s
            sin = base_sin[:, piece] * c + base_cos[:, piece] * s
            upper, lower = halves(jnp.concatenate([cos, sin], 0))
            right = jnp.concatenate([upper, lower, upper], 0)
            total = jnp.dot(left, right, preferred_element_type=jnp.float32)
            out_v[:, :, pl.ds(i * count + j, width)] = total.astype(jnp.bfloat16).reshape(s4, NBLD, width)
        piece = pl.ds(i * count, count)
        copies.append(pltpu.make_async_copy(out_v.at[:, :, piece], out_hbm.at[:, :, piece], out_sem.at[i]))
        copies[-1].start()
    for copy in copies:
        copy.wait()


def inverse(freq_index, wall, s4, hours):
    parts = 8
    return pl.pallas_call(
        functools.partial(inverse_kernel, hours),
        out_shape=jax.ShapeDtypeStruct((s4, NBLD, hours), jnp.bfloat16),
        in_specs=[pl.BlockSpec(memory_space=pltpu.SMEM), pl.BlockSpec(memory_space=pltpu.VMEM)],
        out_specs=pl.BlockSpec(memory_space=pl.ANY),
        scratch_shapes=[
            pltpu.VMEM((s4, NBLD, hours), jnp.bfloat16),
            pltpu.SemaphoreType.DMA((parts,)),
        ],
        compiler_params=pltpu.CompilerParams(vmem_limit_bytes=56 * 2**20),
        name="inverse",
    )(freq_index, pltpu.with_memory_space_constraint(wall, pltpu.VMEM))


def solution(mesh):
    nb, nz = mesh.shape["bore"], mesh.shape["freq"]

    def body(loads, pair_spectra, share, assignment, freq_index):
        owners = assignment.reshape(1, -1)
        wall = superpose(loads, pair_spectra, share, owners, freq_index, nb, nz)
        return inverse(freq_index, wall, loads.shape[0] // nz, loads.shape[2] * nz)

    return jax.shard_map(
        body,
        mesh=mesh,
        in_specs=(
            P("bore", None, "freq"),
            P("freq", None, "bore", None),
            P(None, "bore"),
            P(),
            P(),
        ),
        out_specs=P(("bore", "freq"), None, None),
        check_vma=False,
    )
```

```python
import functools
import math

import jax
import jax.numpy as jnp
from jax import lax
from jax.experimental import pallas as pl
from jax.experimental.pallas import tpu as pltpu
from jax.sharding import PartitionSpec as P

NBLD = 64
FLOC = 2
MESH = pl.DeviceIdType.MESH
NT = (((1,), (1,)), ((), ()))
TN = (((0,), (0,)), ((), ()))


def harmonic_column(freq_ref, freqs):
    row = lax.broadcasted_iota(jnp.int32, (freqs, 1), 0)
    column = jnp.zeros((freqs, 1), jnp.int32)
    for k in range(freqs):
        column = jnp.where(row == k, freq_ref[k], column)
    return column


def cos_sin(harmonics, first_hour, count, hours, stride=1):
    freqs = harmonics.shape[0]
    t = lax.broadcasted_iota(jnp.int32, (freqs, count), 1) * stride + first_hour
    phase = (harmonics * t) & (hours - 1)
    quarter = hours // 4
    turn = (phase + quarter // 2) // quarter
    x = (phase - turn * quarter).astype(jnp.float32) * (2.0 * math.pi / hours)
    y = x * x
    c = 1.0 + y * (-0.5 + y * (1 / 24 + y * (-1 / 720 + y * (1 / 40320 - y * (1 / 3628800)))))
    s = x * (1.0 + y * (-1 / 6 + y * (1 / 120 + y * (-1 / 5040 + y * (1 / 362880)))))
    odd = (turn & 1) == 1
    cos = jnp.where(odd, s, c)
    sin = jnp.where(odd, c, s)
    cos = jnp.where((turn == 1) | (turn == 2), -cos, cos)
    sin = jnp.where((turn == 2) | (turn == 3), -sin, sin)
    return cos, sin


def halves(x):
    upper = x.astype(jnp.bfloat16)
    return upper, (x - upper.astype(jnp.float32)).astype(jnp.bfloat16)


def superpose_kernel(
    nb, nz, hours, freq_ref, owner_ref, loads_hbm, pair_hbm, share_hbm, out_ref,
    loads_v, pair_v, share_v, sel_v, grid_v, cross_stage, cross_recv,
    bs_stage, bs_all, wall_stage, wall_recv,
    loads_sem, pair_sem, own_sem, sh_send, sh_recv, fw_send, fw_recv,
    cr_ssem, cr_rsem, bs_ssem, bs_rsem, wl_ssem, wl_rsem,
):
    b = lax.axis_index("bore")
    z = lax.axis_index("freq")
    sloc = loads_hbm.shape[0]
    tloc = loads_hbm.shape[2]
    freqs = freq_ref.shape[0]
    bores = owner_ref.shape[1]
    bloc = pair_hbm.shape[2]
    scenarios = share_hbm.shape[0]
    s4 = sloc // nz
    core = b % 2
    chip = b // 2
    chips = nb // 2
    sibling = b + 1 - 2 * core
    near_first = sorted(
        ((r, k) for r in range(nb) for k in range(nz) if r or k), key=lambda rk: min(rk[1], nz - rk[1])
    )

    own_share = pltpu.make_async_copy(share_hbm, share_v.at[b], own_sem)
    own_share.start()
    sp = sloc // 2
    hp = tloc // 2
    load_copies = [
        [
            pltpu.make_async_copy(
                loads_hbm.at[pl.ds(i * sp, sp), :, pl.ds(h * hp, hp)],
                loads_v.at[pl.ds(i * sp, sp), :, pl.ds(h * hp, hp)],
                loads_sem.at[i, h],
            )
            for h in range(2)
        ]
        for i in range(2)
    ]
    for copy in load_copies[0] + load_copies[1]:
        copy.start()
    barrier = pltpu.get_barrier_semaphore()
    for r, k in near_first:
        pl.semaphore_signal(barrier, inc=1, device_id=((b + r) % nb, (z + k) % nz), device_id_type=MESH)

    turns = (1 - core, core)
    pair_copies = [
        pltpu.make_async_copy(pair_hbm.at[turns[i], d], pair_v.at[turns[i], d], pair_sem.at[i, d])
        for i in range(FLOC)
        for d in range(2)
    ]

    cos, sin = cos_sin(harmonic_column(freq_ref, freqs), z * tloc, tloc, hours)
    table = jnp.concatenate([*halves(cos), *halves(sin)], 0)
    lanes = sp * NBLD
    square = chips == 4
    over_x = chip + 1 - 2 * (chip % 2)
    over_y = (chip + 2) % chips
    first_hops = (over_x, over_y) if square else tuple((chip + r) % chips for r in range(1, chips))
    first_from = first_hops if square else tuple((chip + chips - r) % chips for r in range(1, chips))
    every = slice(0, scenarios)
    halves_of = [pl.ds(r * (scenarios // 2), scenarios // 2) for r in range(2)]
    if square:
        sends = [(halves_of[r], over) for r, over in enumerate(first_hops)]
        sends += [(halves_of[1 - r], over) for r, over in enumerate(first_hops)]
    else:
        sends = [(every, over) for over in first_hops]
    share_copies = [
        pltpu.make_async_remote_copy(
            src_ref=share_v.at[b, rows], dst_ref=share_v.at[b, rows], send_sem=sh_send.at[r], recv_sem=sh_recv.at[r],
            device_id=device, device_id_type=MESH,
        )
        for r, (rows, device) in enumerate(
            [(rows, (over * 2 + core, z)) for rows, over in sends] + [(every, (sibling, z))]
        )
    ]
    for q in range(nb):
        piece = pl.ds(q * bloc, bloc)
        label = lax.broadcasted_iota(jnp.int32, (2 * NBLD, bloc), 0) % NBLD
        sel_v[:, piece] = (label == owner_ref[:, piece]).astype(jnp.float32).astype(jnp.bfloat16)

    pl.semaphore_wait(barrier, nb * nz - 1)
    own_share.wait()
    for copy in share_copies:
        copy.start()

    folded = []
    for i in range(2):
        spec = jnp.zeros((4 * freqs, lanes), jnp.float32)
        for h in range(2):
            load_copies[i][h].wait()
            pair_copies[2 * i + h].start()
            chunk = loads_v[pl.ds(i * sp, sp), :, pl.ds(h * hp, hp)].reshape(lanes, hp)
            spec = spec + lax.dot_general(
                table[:, h * hp : (h + 1) * hp], chunk, NT, preferred_element_type=jnp.float32
            )
        real = (spec[:freqs] + spec[freqs : 2 * freqs]) * (1.0 / math.sqrt(hours))
        imag = (spec[2 * freqs : 3 * freqs] + spec[3 * freqs :]) * (-1.0 / math.sqrt(hours))
        rows = [
            jnp.concatenate([part[:, r * NBLD : (r + 1) * NBLD] for part in (real, imag)], 1)[None]
            for r in range(sp)
        ]
        folded.append(jnp.swapaxes(jnp.concatenate(rows, 0), 0, 1))
    bs_stage[...] = jnp.concatenate(folded, 1).astype(jnp.bfloat16)

    me = b * nz + z
    others = [j + (me <= j).astype(jnp.int32) for j in range(nb * nz - 1)]

    def spec_copy(to, source):
        return pltpu.make_async_remote_copy(
            src_ref=bs_stage.at[to % nz * FLOC + to // nz % 2], dst_ref=bs_all.at[z, b],
            send_sem=bs_ssem.at[to], recv_sem=bs_rsem.at[source],
            device_id=(to // nz, to % nz), device_id_type=MESH,
        )

    for to in others[::-1]:
        spec_copy(to, me).start()
    bs_all[z, b] = bs_stage[z * FLOC + core]

    here = sel_v[0:NBLD, pl.ds(pl.multiple_of(b * bloc, 128), bloc)]
    width = 2048

    cross_copies = []

    def gather_away(d):
        pair_copies[d].wait()

        def step(i, carry):
            piece = pl.ds(pl.multiple_of(i * width, width), width)
            total = jnp.dot(here, pair_v[turns[0], d, :, piece], preferred_element_type=jnp.float32)
            cross_stage[d, :, piece] = total.astype(jnp.bfloat16)
            return carry

        lax.fori_loop(0, bores // width, step, 0)
        cross_copies.append(
            pltpu.make_async_remote_copy(
                src_ref=cross_stage.at[d], dst_ref=cross_recv.at[d], send_sem=cr_ssem.at[d], recv_sem=cr_rsem.at[d],
                device_id=(sibling, z), device_id_type=MESH,
            )
        )
        cross_copies[-1].start()

    def gather_here(d):
        pair_copies[2 + d].wait()
        cross_copies[d].wait_recv()

        def step(i, carry):
            piece = pl.ds(pl.multiple_of(i * width, width), width)
            total = jnp.dot(here, pair_v[turns[1], d, :, piece], preferred_element_type=jnp.float32)
            total = total + cross_recv[d, :, piece].astype(jnp.float32)
            grid_v[pl.ds(d * NBLD, NBLD), piece] = total.astype(jnp.bfloat16)
            return carry

        lax.fori_loop(0, bores // width, step, 0)

    gather_away(0)

    fw_copies = []

    def forward(r, origin, rows, device):
        there = share_v.at[origin, rows]
        fw_copies.append(
            pltpu.make_async_remote_copy(
                src_ref=there, dst_ref=there, send_sem=fw_send.at[r], recv_sem=fw_recv.at[r],
                device_id=(device, z), device_id_type=MESH,
            )
        )
        fw_copies[-1].start()

    if square:
        for r, origin in enumerate(first_from):
            share_copies[r].wait_recv()
            forward(chips + r, origin * 2 + core, halves_of[r], first_hops[1 - r] * 2 + core)

    gather_away(1)

    gather_here(0)

    for r, origin in enumerate(first_from):
        share_copies[2 + r if square else r].wait_recv()
        forward(r, origin * 2 + core, every, sibling)

    gather_here(1)

    if square:
        diagonal = (over_x + 2) % chips * 2
        for r in range(2):
            fw_copies[r].wait_recv()
        forward(2, diagonal + core, every, sibling)
    share_copies[-1].wait_recv()
    for copy in fw_copies[2:4] if square else fw_copies:
        copy.wait_recv()
    half = lax.broadcasted_iota(jnp.int32, (scenarios // 2, 128), 1) // NBLD
    sign = jnp.where(lax.broadcasted_iota(jnp.int32, (scenarios // 2, 128), 1) < NBLD, -1.0, 1.0)
    slot = z * FLOC + core

    def wall_copy(to, source):
        return pltpu.make_async_remote_copy(
            src_ref=wall_stage.at[to], dst_ref=wall_recv.at[slot, chip],
            send_sem=wl_ssem.at[to], recv_sem=wl_rsem.at[source],
            device_id=(to // nz, to % nz), device_id_type=MESH,
        )

    def source_blocks(part, spec_c, origins, walls):
        rows = slice(part * (scenarios // 2), (part + 1) * (scenarios // 2))
        for q in origins:
            piece = pl.ds(pl.multiple_of(q * bloc, 128), bloc)
            weight = share_v[q, rows].astype(jnp.float32)
            picked = jnp.dot(spec_c, sel_v[:, piece], preferred_element_type=jnp.float32)
            source = (picked.reshape(2, scenarios // 2, bloc) * weight).astype(jnp.bfloat16).reshape(scenarios, bloc)
            walls = walls + lax.dot_general(source, grid_v[:, piece], NT, preferred_element_type=jnp.float32)
        return walls

    mid = nb * nz // 2
    for part in range(2):
        for other in others[mid:] if part else others[:mid]:
            spec_copy(other, other).wait_recv()
        blocks = slice(part * (nb // 2), (part + 1) * (nb // 2))
        spec = bs_all[0, blocks].astype(jnp.float32)
        for k in range(1, nz):
            spec = spec + bs_all[k, blocks].astype(jnp.float32)
        spec = spec.reshape(scenarios // 2, 128)
        spec_c = jnp.concatenate([jnp.where(half == c, spec, 0.0).astype(jnp.bfloat16) for c in range(2)], 0)
        walls = jnp.zeros((scenarios, 128), jnp.float32)
        if square and part == 0:
            near = [q * 2 + c for q in (chip, over_x, over_y) for c in range(2)]
            walls = source_blocks(part, spec_c, [*near, diagonal + core], walls)
            fw_copies[4].wait_recv()
            walls = source_blocks(part, spec_c, [diagonal + 1 - core], walls)
        else:
            walls = source_blocks(part, spec_c, range(nb), walls)
        joined = walls[: scenarios // 2] + sign * pltpu.roll(walls[scenarios // 2 :], NBLD, 1)
        wall_stage[pl.ds(part * mid, mid)] = (joined * (NBLD / bores)).reshape(mid, s4, 128)
        for to in others[mid - 1 :] if part else others[: mid - 1]:
            wall_copy(to, me).start()
    wall_recv[slot, chip] = wall_stage[b * nz + z]
    for other in others:
        spec_copy(other, other).wait_send()
    for copy in share_copies + fw_copies + cross_copies:
        copy.wait_send()
    for other in others:
        wall_copy(other, other).wait()
    wall = wall_recv[:, 0]
    for q in range(1, chips):
        wall = wall + wall_recv[:, q]
    out_ref[...] = wall.reshape(freqs * s4, 128)


def superpose(loads, pair_spectra, share, owners, freq_index, nb, nz):
    sloc, _, tloc = loads.shape
    bloc, bores = pair_spectra.shape[2:]
    scenarios = share.shape[0]
    freqs = freq_index.shape[0]
    s4 = sloc // nz
    bf16, f32, dma = jnp.bfloat16, jnp.float32, pltpu.SemaphoreType.DMA
    anywhere = pl.BlockSpec(memory_space=pl.ANY)
    return pl.pallas_call(
        functools.partial(superpose_kernel, nb, nz, tloc * nz),
        out_shape=pltpu.VMEM((nz * FLOC * s4, 128), f32),
        in_specs=[
            pl.BlockSpec(memory_space=pltpu.SMEM),
            pl.BlockSpec(memory_space=pltpu.VMEM),
            anywhere,
            anywhere,
            anywhere,
        ],
        out_specs=pl.BlockSpec(memory_space=pltpu.VMEM),
        scratch_shapes=[
            pltpu.VMEM(loads.shape, bf16),
            pltpu.VMEM(pair_spectra.shape, bf16),
            pltpu.VMEM((nb, scenarios, bloc), bf16),
            pltpu.VMEM((2 * NBLD, bores), bf16),
            pltpu.VMEM((2 * NBLD, bores), bf16),
            pltpu.VMEM((2, NBLD, bores), bf16),
            pltpu.VMEM((2, NBLD, bores), bf16),
            pltpu.VMEM((freqs, sloc, 128), bf16),
            pltpu.VMEM((nz, nb, sloc, 128), bf16),
            pltpu.VMEM((nb * nz, s4, 128), f32),
            pltpu.VMEM((freqs, nb // 2, s4, 128), f32),
            dma((2, 2)),
            dma((FLOC, 2)),
            dma,
            dma((nb // 2 + 1,)),
            dma((nb // 2 + 1,)),
            dma((nb // 2 + 2,)),
            dma((nb // 2 + 2,)),
            dma((2,)),
            dma((2,)),
            dma((nb * nz,)),
            dma((nb * nz,)),
            dma((nb * nz,)),
            dma((nb * nz,)),
        ],
        compiler_params=pltpu.CompilerParams(
            collective_id=0, has_side_effects=True, vmem_limit_bytes=56 * 2**20
        ),
        name="superpose",
    )(freq_index, owners, loads, pair_spectra, share)


def inverse_kernel(hours, freq_ref, wall_v, out_hbm, out_v, out_sem):
    freqs = freq_ref.shape[0]
    s4 = out_hbm.shape[0]
    parts = out_sem.shape[0]
    count = hours // parts
    harmonics = harmonic_column(freq_ref, freqs)
    base_cos, base_sin = cos_sin(harmonics, 0, count, hours)
    turn_cos, turn_sin = cos_sin(harmonics, 0, 128, hours, count)
    low = lax.broadcasted_iota(jnp.int32, (freqs, 128), 1) < NBLD
    real, imag = [], []
    for s in range(0, s4, 2):
        one = wall_v[pl.ds(s, freqs, stride=s4), :]
        two = wall_v[pl.ds(s + 1, freqs, stride=s4), :]
        real.append(jnp.where(low, one, pltpu.roll(two, NBLD, 1)))
        imag.append(jnp.where(low, pltpu.roll(one, NBLD, 1), two))
    left = jnp.concatenate([jnp.concatenate(real, 1), -jnp.concatenate(imag, 1)], 0)
    upper, lower = halves(left * (1.0 / math.sqrt(freqs)))
    upper, lower = upper.astype(jnp.float32), lower.astype(jnp.float32)
    left = jnp.concatenate([upper, upper, lower], 0).T.astype(jnp.bfloat16)
    width = min(512, count)
    copies = []
    for i in range(parts):
        c, s = turn_cos[:, i : i + 1], turn_sin[:, i : i + 1]
        for j in range(0, count, width):
            piece = slice(j, j + width)
            cos = base_cos[:, piece] * c - base_sin[:, piece] * s
            sin = base_sin[:, piece] * c + base_cos[:, piece] * s
            upper, lower = halves(jnp.concatenate([cos, sin], 0))
            right = jnp.concatenate([upper, lower, upper], 0)
            total = jnp.dot(left, right, preferred_element_type=jnp.float32)
            out_v[:, :, pl.ds(i * count + j, width)] = total.astype(jnp.bfloat16).reshape(s4, NBLD, width)
        piece = pl.ds(i * count, count)
        copies.append(pltpu.make_async_copy(out_v.at[:, :, piece], out_hbm.at[:, :, piece], out_sem.at[i]))
        copies[-1].start()
    for copy in copies:
        copy.wait()


def inverse(freq_index, wall, s4, hours):
    parts = 8
    return pl.pallas_call(
        functools.partial(inverse_kernel, hours),
        out_shape=jax.ShapeDtypeStruct((s4, NBLD, hours), jnp.bfloat16),
        in_specs=[pl.BlockSpec(memory_space=pltpu.SMEM), pl.BlockSpec(memory_space=pltpu.VMEM)],
        out_specs=pl.BlockSpec(memory_space=pl.ANY),
        scratch_shapes=[
            pltpu.VMEM((s4, NBLD, hours), jnp.bfloat16),
            pltpu.SemaphoreType.DMA((parts,)),
        ],
        compiler_params=pltpu.CompilerParams(vmem_limit_bytes=56 * 2**20),
        name="inverse",
    )(freq_index, pltpu.with_memory_space_constraint(wall, pltpu.VMEM))


def solution(mesh):
    nb, nz = mesh.shape["bore"], mesh.shape["freq"]

    def body(loads, pair_spectra, share, assignment, freq_index):
        owners = assignment.reshape(1, -1)
        wall = superpose(loads, pair_spectra, share, owners, freq_index, nb, nz)
        return inverse(freq_index, wall, loads.shape[0] // nz, loads.shape[2] * nz)

    return jax.shard_map(
        body,
        mesh=mesh,
        in_specs=(
            P("bore", None, "freq"),
            P("freq", None, "bore", None),
            P(None, "bore"),
            P(),
            P(),
        ),
        out_specs=P(("bore", "freq"), None, None),
        check_vma=False,
    )
```

```python
import functools
import math

import jax
import jax.numpy as jnp
from jax import lax
from jax.experimental import pallas as pl
from jax.experimental.pallas import tpu as pltpu
from jax.sharding import PartitionSpec as P

NBLD = 64
FLOC = 2
MESH = pl.DeviceIdType.MESH
NT = (((1,), (1,)), ((), ()))
TN = (((0,), (0,)), ((), ()))


def harmonic_column(freq_ref, freqs):
    row = lax.broadcasted_iota(jnp.int32, (freqs, 1), 0)
    column = jnp.zeros((freqs, 1), jnp.int32)
    for k in range(freqs):
        column = jnp.where(row == k, freq_ref[k], column)
    return column


def cos_sin(harmonics, first_hour, count, hours, stride=1):
    freqs = harmonics.shape[0]
    t = lax.broadcasted_iota(jnp.int32, (freqs, count), 1) * stride + first_hour
    phase = (harmonics * t) & (hours - 1)
    quarter = hours // 4
    turn = (phase + quarter // 2) // quarter
    x = (phase - turn * quarter).astype(jnp.float32) * (2.0 * math.pi / hours)
    y = x * x
    c = 1.0 + y * (-0.5 + y * (1 / 24 + y * (-1 / 720 + y * (1 / 40320 - y * (1 / 3628800)))))
    s = x * (1.0 + y * (-1 / 6 + y * (1 / 120 + y * (-1 / 5040 + y * (1 / 362880)))))
    odd = (turn & 1) == 1
    cos = jnp.where(odd, s, c)
    sin = jnp.where(odd, c, s)
    cos = jnp.where((turn == 1) | (turn == 2), -cos, cos)
    sin = jnp.where((turn == 2) | (turn == 3), -sin, sin)
    return cos, sin


def halves(x):
    upper = x.astype(jnp.bfloat16)
    return upper, (x - upper.astype(jnp.float32)).astype(jnp.bfloat16)


def superpose_kernel(
    nb, nz, hours, freq_ref, owner_ref, loads_hbm, pair_hbm, share_hbm, out_ref,
    loads_v, pair_v, share_v, sel_v, grid_v, cross_stage, cross_recv,
    bs_stage, bs_all, wall_stage, wall_recv,
    loads_sem, pair_sem, own_sem, sh_send, sh_recv, fw_send, fw_recv,
    cr_ssem, cr_rsem, bs_ssem, bs_rsem, wl_ssem, wl_rsem,
):
    b = lax.axis_index("bore")
    z = lax.axis_index("freq")
    sloc = loads_hbm.shape[0]
    tloc = loads_hbm.shape[2]
    freqs = freq_ref.shape[0]
    bores = owner_ref.shape[1]
    bloc = pair_hbm.shape[2]
    scenarios = share_hbm.shape[0]
    s4 = sloc // nz
    core = b % 2
    chip = b // 2
    chips = nb // 2
    sibling = b + 1 - 2 * core
    near_first = sorted(
        ((r, k) for r in range(nb) for k in range(nz) if r or k), key=lambda rk: min(rk[1], nz - rk[1])
    )

    own_share = pltpu.make_async_copy(share_hbm, share_v.at[b], own_sem)
    own_share.start()
    sp = sloc // 2
    hp = tloc // 2
    load_copies = [
        [
            pltpu.make_async_copy(
                loads_hbm.at[pl.ds(i * sp, sp), :, pl.ds(h * hp, hp)],
                loads_v.at[pl.ds(i * sp, sp), :, pl.ds(h * hp, hp)],
                loads_sem.at[i, h],
            )
            for h in range(2)
        ]
        for i in range(2)
    ]
    for copy in load_copies[0] + load_copies[1]:
        copy.start()
    barrier = pltpu.get_barrier_semaphore()
    for r, k in near_first:
        pl.semaphore_signal(barrier, inc=1, device_id=((b + r) % nb, (z + k) % nz), device_id_type=MESH)

    turns = (1 - core, core)
    pair_copies = [
        pltpu.make_async_copy(pair_hbm.at[turns[i], d], pair_v.at[turns[i], d], pair_sem.at[i, d])
        for i in range(FLOC)
        for d in range(2)
    ]

    cos, sin = cos_sin(harmonic_column(freq_ref, freqs), z * tloc, tloc, hours)
    table = jnp.concatenate([*halves(cos), *halves(sin)], 0)
    lanes = sp * NBLD
    square = chips == 4
    over_x = chip + 1 - 2 * (chip % 2)
    over_y = (chip + 2) % chips
    first_hops = (over_x, over_y) if square else tuple((chip + r) % chips for r in range(1, chips))
    first_from = first_hops if square else tuple((chip + chips - r) % chips for r in range(1, chips))
    every = slice(0, scenarios)
    halves_of = [pl.ds(r * (scenarios // 2), scenarios // 2) for r in range(2)]
    if square:
        sends = [(halves_of[r], over) for r, over in enumerate(first_hops)]
        sends += [(halves_of[1 - r], over) for r, over in enumerate(first_hops)]
    else:
        sends = [(every, over) for over in first_hops]
    share_copies = [
        pltpu.make_async_remote_copy(
            src_ref=share_v.at[b, rows], dst_ref=share_v.at[b, rows], send_sem=sh_send.at[r], recv_sem=sh_recv.at[r],
            device_id=device, device_id_type=MESH,
        )
        for r, (rows, device) in enumerate(
            [(rows, (over * 2 + core, z)) for rows, over in sends] + [(every, (sibling, z))]
        )
    ]
    for q in range(nb):
        piece = pl.ds(q * bloc, bloc)
        label = lax.broadcasted_iota(jnp.int32, (2 * NBLD, bloc), 0) % NBLD
        sel_v[:, piece] = (label == owner_ref[:, piece]).astype(jnp.float32).astype(jnp.bfloat16)

    pl.semaphore_wait(barrier, nb * nz - 1)
    own_share.wait()
    for copy in share_copies:
        copy.start()

    folded = []
    for i in range(2):
        spec = jnp.zeros((4 * freqs, lanes), jnp.float32)
        for h in range(2):
            load_copies[i][h].wait()
            pair_copies[2 * i + h].start()
            chunk = loads_v[pl.ds(i * sp, sp), :, pl.ds(h * hp, hp)].reshape(lanes, hp)
            spec = spec + lax.dot_general(
                table[:, h * hp : (h + 1) * hp], chunk, NT, preferred_element_type=jnp.float32
            )
        real = (spec[:freqs] + spec[freqs : 2 * freqs]) * (1.0 / math.sqrt(hours))
        imag = (spec[2 * freqs : 3 * freqs] + spec[3 * freqs :]) * (-1.0 / math.sqrt(hours))
        rows = [
            jnp.concatenate([part[:, r * NBLD : (r + 1) * NBLD] for part in (real, imag)], 1)[None]
            for r in range(sp)
        ]
        folded.append(jnp.swapaxes(jnp.concatenate(rows, 0), 0, 1))
    bs_stage[...] = jnp.concatenate(folded, 1).astype(jnp.bfloat16)

    me = b * nz + z
    others = [j + (me <= j).astype(jnp.int32) for j in range(nb * nz - 1)]

    def spec_copy(to, source):
        return pltpu.make_async_remote_copy(
            src_ref=bs_stage.at[to % nz * FLOC + to // nz % 2], dst_ref=bs_all.at[z, b],
            send_sem=bs_ssem.at[to], recv_sem=bs_rsem.at[source],
            device_id=(to // nz, to % nz), device_id_type=MESH,
        )

    for to in others[::-1]:
        spec_copy(to, me).start()
    bs_all[z, b] = bs_stage[z * FLOC + core]

    here = sel_v[0:NBLD, pl.ds(pl.multiple_of(b * bloc, 128), bloc)]
    width = 4096

    cross_copies = []

    def gather_away(d):
        pair_copies[d].wait()

        def step(i, carry):
            piece = pl.ds(pl.multiple_of(i * width, width), width)
            total = jnp.dot(here, pair_v[turns[0], d, :, piece], preferred_element_type=jnp.float32)
            cross_stage[d, :, piece] = total.astype(jnp.bfloat16)
            return carry

        lax.fori_loop(0, bores // width, step, 0)
        cross_copies.append(
            pltpu.make_async_remote_copy(
                src_ref=cross_stage.at[d], dst_ref=cross_recv.at[d], send_sem=cr_ssem.at[d], recv_sem=cr_rsem.at[d],
                device_id=(sibling, z), device_id_type=MESH,
            )
        )
        cross_copies[-1].start()

    def gather_here(d):
        pair_copies[2 + d].wait()
        cross_copies[d].wait_recv()

        def step(i, carry):
            piece = pl.ds(pl.multiple_of(i * width, width), width)
            total = jnp.dot(here, pair_v[turns[1], d, :, piece], preferred_element_type=jnp.float32)
            total = total + cross_recv[d, :, piece].astype(jnp.float32)
            grid_v[pl.ds(d * NBLD, NBLD), piece] = total.astype(jnp.bfloat16)
            return carry

        lax.fori_loop(0, bores // width, step, 0)

    gather_away(0)

    fw_copies = []

    def forward(r, origin, rows, device):
        there = share_v.at[origin, rows]
        fw_copies.append(
            pltpu.make_async_remote_copy(
                src_ref=there, dst_ref=there, send_sem=fw_send.at[r], recv_sem=fw_recv.at[r],
                device_id=(device, z), device_id_type=MESH,
            )
        )
        fw_copies[-1].start()

    if square:
        for r, origin in enumerate(first_from):
            share_copies[r].wait_recv()
            forward(chips + r, origin * 2 + core, halves_of[r], first_hops[1 - r] * 2 + core)

    gather_away(1)

    gather_here(0)

    for r, origin in enumerate(first_from):
        share_copies[2 + r if square else r].wait_recv()
        forward(r, origin * 2 + core, every, sibling)

    gather_here(1)

    if square:
        diagonal = (over_x + 2) % chips * 2
        fw_copies[0].wait_recv()
        forward(2, diagonal + core, halves_of[0], sibling)
    share_copies[-1].wait_recv()
    for copy in fw_copies[2:4] if square else fw_copies:
        copy.wait_recv()
    half = lax.broadcasted_iota(jnp.int32, (scenarios // 2, 128), 1) // NBLD
    sign = jnp.where(lax.broadcasted_iota(jnp.int32, (scenarios // 2, 128), 1) < NBLD, -1.0, 1.0)
    slot = z * FLOC + core

    def wall_copy(to, source):
        return pltpu.make_async_remote_copy(
            src_ref=wall_stage.at[to], dst_ref=wall_recv.at[slot, chip],
            send_sem=wl_ssem.at[to], recv_sem=wl_rsem.at[source],
            device_id=(to // nz, to % nz), device_id_type=MESH,
        )

    def source_blocks(part, spec_c, origins, walls):
        rows = slice(part * (scenarios // 2), (part + 1) * (scenarios // 2))
        for q in origins:
            piece = pl.ds(pl.multiple_of(q * bloc, 128), bloc)
            weight = share_v[q, rows].astype(jnp.float32)
            picked = jnp.dot(spec_c, sel_v[:, piece], preferred_element_type=jnp.float32)
            source = (picked.reshape(2, scenarios // 2, bloc) * weight).astype(jnp.bfloat16).reshape(scenarios, bloc)
            walls = walls + lax.dot_general(source, grid_v[:, piece], NT, preferred_element_type=jnp.float32)
        return walls

    mid = nb * nz // 2
    for part in range(2):
        for other in others[mid:] if part else others[:mid]:
            spec_copy(other, other).wait_recv()
        blocks = slice(part * (nb // 2), (part + 1) * (nb // 2))
        spec = bs_all[0, blocks].astype(jnp.float32)
        for k in range(1, nz):
            spec = spec + bs_all[k, blocks].astype(jnp.float32)
        spec = spec.reshape(scenarios // 2, 128)
        spec_c = jnp.concatenate([jnp.where(half == c, spec, 0.0).astype(jnp.bfloat16) for c in range(2)], 0)
        walls = jnp.zeros((scenarios, 128), jnp.float32)
        if square and part == 0:
            near = [q * 2 + c for q in (chip, over_x, over_y) for c in range(2)]
            walls = source_blocks(part, spec_c, [*near, diagonal + core], walls)
            fw_copies[1].wait_recv()
            forward(3, diagonal + core, halves_of[1], sibling)
            fw_copies[4].wait_recv()
            walls = source_blocks(part, spec_c, [diagonal + 1 - core], walls)
        else:
            if square:
                fw_copies[5].wait_recv()
            walls = source_blocks(part, spec_c, range(nb), walls)
        joined = walls[: scenarios // 2] + sign * pltpu.roll(walls[scenarios // 2 :], NBLD, 1)
        wall_stage[pl.ds(part * mid, mid)] = (joined * (NBLD / bores)).reshape(mid, s4, 128)
        for to in others[mid - 1 :] if part else others[: mid - 1]:
            wall_copy(to, me).start()
    wall_recv[slot, chip] = wall_stage[b * nz + z]
    for other in others:
        spec_copy(other, other).wait_send()
    for copy in share_copies + fw_copies + cross_copies:
        copy.wait_send()
    for other in others:
        wall_copy(other, other).wait()
    wall = wall_recv[:, 0]
    for q in range(1, chips):
        wall = wall + wall_recv[:, q]
    out_ref[...] = wall.reshape(freqs * s4, 128)


def superpose(loads, pair_spectra, share, owners, freq_index, nb, nz):
    sloc, _, tloc = loads.shape
    bloc, bores = pair_spectra.shape[2:]
    scenarios = share.shape[0]
    freqs = freq_index.shape[0]
    s4 = sloc // nz
    bf16, f32, dma = jnp.bfloat16, jnp.float32, pltpu.SemaphoreType.DMA
    anywhere = pl.BlockSpec(memory_space=pl.ANY)
    return pl.pallas_call(
        functools.partial(superpose_kernel, nb, nz, tloc * nz),
        out_shape=pltpu.VMEM((nz * FLOC * s4, 128), f32),
        in_specs=[
            pl.BlockSpec(memory_space=pltpu.SMEM),
            pl.BlockSpec(memory_space=pltpu.VMEM),
            anywhere,
            anywhere,
            anywhere,
        ],
        out_specs=pl.BlockSpec(memory_space=pltpu.VMEM),
        scratch_shapes=[
            pltpu.VMEM(loads.shape, bf16),
            pltpu.VMEM(pair_spectra.shape, bf16),
            pltpu.VMEM((nb, scenarios, bloc), bf16),
            pltpu.VMEM((2 * NBLD, bores), bf16),
            pltpu.VMEM((2 * NBLD, bores), bf16),
            pltpu.VMEM((2, NBLD, bores), bf16),
            pltpu.VMEM((2, NBLD, bores), bf16),
            pltpu.VMEM((freqs, sloc, 128), bf16),
            pltpu.VMEM((nz, nb, sloc, 128), bf16),
            pltpu.VMEM((nb * nz, s4, 128), f32),
            pltpu.VMEM((freqs, nb // 2, s4, 128), f32),
            dma((2, 2)),
            dma((FLOC, 2)),
            dma,
            dma((nb // 2 + 1,)),
            dma((nb // 2 + 1,)),
            dma((nb // 2 + 2,)),
            dma((nb // 2 + 2,)),
            dma((2,)),
            dma((2,)),
            dma((nb * nz,)),
            dma((nb * nz,)),
            dma((nb * nz,)),
            dma((nb * nz,)),
        ],
        compiler_params=pltpu.CompilerParams(
            collective_id=0, has_side_effects=True, vmem_limit_bytes=56 * 2**20
        ),
        name="superpose",
    )(freq_index, owners, loads, pair_spectra, share)


def inverse_kernel(hours, freq_ref, wall_v, out_hbm, out_v, out_sem):
    freqs = freq_ref.shape[0]
    s4 = out_hbm.shape[0]
    parts = out_sem.shape[0]
    count = hours // parts
    harmonics = harmonic_column(freq_ref, freqs)
    base_cos, base_sin = cos_sin(harmonics, 0, count, hours)
    turn_cos, turn_sin = cos_sin(harmonics, 0, 128, hours, count)
    low = lax.broadcasted_iota(jnp.int32, (freqs, 128), 1) < NBLD
    real, imag = [], []
    for s in range(0, s4, 2):
        one = wall_v[pl.ds(s, freqs, stride=s4), :]
        two = wall_v[pl.ds(s + 1, freqs, stride=s4), :]
        real.append(jnp.where(low, one, pltpu.roll(two, NBLD, 1)))
        imag.append(jnp.where(low, pltpu.roll(one, NBLD, 1), two))
    left = jnp.concatenate([jnp.concatenate(real, 1), -jnp.concatenate(imag, 1)], 0)
    upper, lower = halves(left * (1.0 / math.sqrt(freqs)))
    upper, lower = upper.astype(jnp.float32), lower.astype(jnp.float32)
    left = jnp.concatenate([upper, upper, lower], 0).T.astype(jnp.bfloat16)
    width = min(512, count)
    copies = []
    for i in range(parts):
        c, s = turn_cos[:, i : i + 1], turn_sin[:, i : i + 1]
        for j in range(0, count, width):
            piece = slice(j, j + width)
            cos = base_cos[:, piece] * c - base_sin[:, piece] * s
            sin = base_sin[:, piece] * c + base_cos[:, piece] * s
            upper, lower = halves(jnp.concatenate([cos, sin], 0))
            right = jnp.concatenate([upper, lower, upper], 0)
            total = jnp.dot(left, right, preferred_element_type=jnp.float32)
            out_v[:, :, pl.ds(i * count + j, width)] = total.astype(jnp.bfloat16).reshape(s4, NBLD, width)
        piece = pl.ds(i * count, count)
        copies.append(pltpu.make_async_copy(out_v.at[:, :, piece], out_hbm.at[:, :, piece], out_sem.at[i]))
        copies[-1].start()
    for copy in copies:
        copy.wait()


def inverse(freq_index, wall, s4, hours):
    parts = 8
    return pl.pallas_call(
        functools.partial(inverse_kernel, hours),
        out_shape=jax.ShapeDtypeStruct((s4, NBLD, hours), jnp.bfloat16),
        in_specs=[pl.BlockSpec(memory_space=pltpu.SMEM), pl.BlockSpec(memory_space=pltpu.VMEM)],
        out_specs=pl.BlockSpec(memory_space=pl.ANY),
        scratch_shapes=[
            pltpu.VMEM((s4, NBLD, hours), jnp.bfloat16),
            pltpu.SemaphoreType.DMA((parts,)),
        ],
        compiler_params=pltpu.CompilerParams(vmem_limit_bytes=56 * 2**20),
        name="inverse",
    )(freq_index, pltpu.with_memory_space_constraint(wall, pltpu.VMEM))


def solution(mesh):
    nb, nz = mesh.shape["bore"], mesh.shape["freq"]

    def body(loads, pair_spectra, share, assignment, freq_index):
        owners = assignment.reshape(1, -1)
        wall = superpose(loads, pair_spectra, share, owners, freq_index, nb, nz)
        return inverse(freq_index, wall, loads.shape[0] // nz, loads.shape[2] * nz)

    return jax.shard_map(
        body,
        mesh=mesh,
        in_specs=(
            P("bore", None, "freq"),
            P("freq", None, "bore", None),
            P(None, "bore"),
            P(),
            P(),
        ),
        out_specs=P(("bore", "freq"), None, None),
        check_vma=False,
    )
```
